256 devices in a mesh: row: 32 (over x, y, core), col: 8 (over z).
Axes of the slice: x: 4, y: 4, z: 8, core: 2. Of those that a mesh axis runs over, the one named last changes fastest.
Arguments:
- tokens: bfloat16 [1024, 8192], P('row', 'col'), may hold values from -6 to 6
- cotangent: bfloat16 [1024, 8192], P('row', 'col'), may hold values from -1.5 to 1.5
- gate_weight: bfloat16 [8192, 16384], P('col', 'row'), may hold values from -0.0625 to 0.0625
- up_weight: bfloat16 [8192, 16384], P('col', 'row'), may hold values from -0.0625 to 0.0625
- down_weight: bfloat16 [16384, 8192], P('row', 'col'), may hold values from -0.046875 to 0.046875
Outputs:
- grad_gate: bfloat16 [8192, 16384], P('col', 'row')
- grad_up: bfloat16 [8192, 16384], P('col', 'row')
- grad_down: bfloat16 [16384, 8192], P('row', 'col')
- grad_input: bfloat16 [1024, 8192], P('row', 'col')
The draws below stay inside these ranges and needn't reach their ends.
All inputs are finite; a program needn't handle non-finite values.
Results may differ from the reference program's by a relative error of at most 0.0049.
Values may be sent and summed in bfloat16 or wider, within the bound.
A program may use at most 64 MiB of HBM per device.

```python
import jax
import jax.numpy as jnp

D = 8192
FF = 16384
TOKENS = 1024


def level_of(stream_key, extent, split, smallest, largest):
    factor_of = 1.0
    for position, shards_of in split:
        heights = jax.random.uniform(jax.random.fold_in(jax.random.fold_in(stream_key, 6), position), (shards_of,), jnp.float32, smallest / len(split), largest / len(split))
        factor_of = factor_of * jnp.repeat(jnp.exp(heights), extent[position] // shards_of).reshape((-1,) + (1,) * (len(extent) - 1 - position))
    return factor_of


def normal_values(stream_key, dims, scale, reach, shards=(), dtype=jnp.bfloat16):
    factor_of = level_of(stream_key, dims, shards, -0.22, 0.18) if shards else 1.0
    drawn = jax.random.normal(stream_key, dims, jnp.float32) * scale * factor_of
    return jnp.minimum(jnp.maximum(drawn, -reach), reach).astype(dtype)


def setup_inputs(seed: int = 0) -> dict:
    key_of = jax.random.split(jax.random.key(seed), 6)
    return {
        "tokens": normal_values(key_of[0], (TOKENS, D), 1.0, 6.0, ((0, 32), (1, 8))),
        "cotangent": normal_values(key_of[1], (TOKENS, D), 0.25, 1.5, ((0, 32), (1, 8))),
        "gate_weight": normal_values(key_of[2], (D, FF), D ** -0.5, 0.0625, ((0, 8), (1, 32))),
        "up_weight": normal_values(key_of[3], (D, FF), D ** -0.5, 0.0625, ((0, 8), (1, 32))),
        "down_weight": normal_values(key_of[4], (FF, D), FF ** -0.5, 0.046875, ((0, 32), (1, 8))),
    }


def swiglu_back(gate, up, back):
    sig = jax.nn.sigmoid(gate)
    hidden = (gate * sig * up).astype(jnp.bfloat16)
    gate_grad = (back * up * sig * (1.0 + gate * (1.0 - sig))).astype(jnp.bfloat16)
    up_grad = (back * gate * sig).astype(jnp.bfloat16)
    return hidden, gate_grad, up_grad


def reference(tokens, cotangent, gate_weight, up_weight, down_weight):
    gate = jnp.dot(tokens, gate_weight, preferred_element_type=jnp.float32)
    up = jnp.dot(tokens, up_weight, preferred_element_type=jnp.float32)
    back = jnp.dot(cotangent, down_weight.T, preferred_element_type=jnp.float32)
    hidden, gate_grad, up_grad = swiglu_back(gate, up, back)
    grad_down = jnp.dot(hidden.T, cotangent, preferred_element_type=jnp.float32).astype(jnp.bfloat16)
    grad_gate = jnp.dot(tokens.T, gate_grad, preferred_element_type=jnp.float32).astype(jnp.bfloat16)
    grad_up = jnp.dot(tokens.T, up_grad, preferred_element_type=jnp.float32).astype(jnp.bfloat16)
    input_total = jnp.dot(gate_grad, gate_weight.T, preferred_element_type=jnp.float32)
    input_total = input_total + jnp.dot(up_grad, up_weight.T, preferred_element_type=jnp.float32)
    return grad_gate, grad_up, grad_down, input_total.astype(jnp.bfloat16)
```

```python
import jax
import jax.numpy as jnp
from jax import lax
from jax.experimental import pallas as pl
from jax.experimental.pallas import tpu as pltpu
from jax.sharding import PartitionSpec as P

MESH = pl.DeviceIdType.MESH
F32, BF16 = jnp.float32, jnp.bfloat16
INNER = (((1,), (1,)), ((), ()))
OUTER = (((0,), (0,)), ((), ()))
SCALE = 2.0**51
LANES = ((0, 256), (256, 256))


def encode(value):
    scaled = value * SCALE
    return (scaled * jnp.abs(scaled)).astype(BF16)


def decode(coded):
    wide = coded.astype(F32)
    return wide * lax.rsqrt(jnp.maximum(jnp.abs(wide), 1e-37)) * (1.0 / SCALE)


def product(a, b, dims=(((1,), (0,)), ((), ()))):
    return lax.dot_general(a, b, dims, preferred_element_type=F32)


def kernel(
    tok_ref, cot_ref, wg_ref, wu_ref, wd_ref,
    gg_ref, gu_ref, gd_ref, gi_ref,
    rows, part, sent, got, hid, acc, accd, give, take, out16, in16, local,
    rows_s, rows_r, pair_s, pair_r, red_s, red_r, gat_s, gat_r, give_s, give_r, gi_s, gi_r,
):
    row, z = lax.axis_index("row"), lax.axis_index("col")
    x, y, c = row // 8, (row // 2) % 4, row % 2

    def at(px, py, pc):
        return ((px % 4) * 4 + (py % 4)) * 2 + pc

    partner = (at(x, y, 1 - c), z)
    side = ((row, (z + 1) % 8), (row, (z + 7) % 8))

    def remote(src, dst, s, r, device):
        return pltpu.make_async_remote_copy(
            src_ref=src, dst_ref=dst, send_sem=s, recv_sem=r, device_id=device, device_id_type=MESH
        )

    barrier = pltpu.get_barrier_semaphore()
    peers = [side[0], side[1], partner]
    peers += [(at(x + k, y + d, c), z) for k in range(4) for d in range(4) if (k, d) != (0, 0)]
    for peer in peers:
        pl.semaphore_signal(barrier, inc=1, device_id=peer, device_id_type=MESH)
    pl.semaphore_wait(barrier, len(peers))

    mine = pl.ds(pl.multiple_of(y * 32, 32), 32)
    sources = (tok_ref, cot_ref)

    def rows_copy(a, k, d):
        return remote(
            sources[a], rows.at[a, x, c, mine], rows_s.at[a, k, d], rows_r.at[a, k, d], (at(x - k, y - d, c), z)
        )

    def rows_send(k):
        for d in (0, 1, 3, 2):
            if (k, d) != (0, 0):
                for a in range(2):
                    rows_copy(a, k, d).start()

    def rows_wait(k):
        for d in range(4):
            if (k, d) != (0, 0):
                for a in range(2):
                    place = pl.ds(pl.multiple_of(((y + d) % 4) * 32, 32), 32)
                    ref = rows.at[a, (x + k) % 4, c, place]
                    remote(ref, ref, rows_s.at[a, k, d], rows_r.at[a, k, d], partner).wait_recv()

    def pair_copy(a, j, core):
        ref = rows.at[a, (x + j) % 4, core]
        return remote(ref, ref, pair_s.at[a, j], pair_r.at[a, j], partner)

    def pair_send(j):
        for a in range(2):
            pair_copy(a, j, c).start()

    def pair_wait(j):
        for a in range(2):
            pair_copy(a, j, 1 - c).wait_recv()

    def block(o):
        return pl.ds(pl.multiple_of((o % 8) * 16, 16), 16)

    def red_copy(s, way, h):
        if h == 0:
            lanes = pl.ds(*LANES[way])
            src, dst = sent.at[s, way, h, :, :, :, lanes], got.at[s, way, h, :, :, :, lanes]
        else:
            src, dst = sent.at[s, way, h], got.at[s, way, h]
        return remote(src, dst, red_s.at[s, way, h], red_r.at[s, way, h], side[way])

    def red_first(s):
        for way in range(2):
            lanes = pl.ds(*LANES[way])
            sent[s, way, 0, :, :, :, lanes] = encode(part[:, s, :, block(z + 4), lanes])
            red_copy(s, way, 0).start()

    def red_hop(s, h):
        for way in range(2):
            o = z + 4 - h if way == 0 else z + 4 + h
            red_copy(s, way, h - 1).wait_recv()
            for q in range(3):
                if h == 1:
                    for w in range(2):
                        lanes = pl.ds(*LANES[w])
                        value = part[q, s, :, block(o), lanes]
                        if w == way:
                            value = value + decode(got[s, way, 0, q, :, :, lanes])
                        sent[s, way, h, q, :, :, lanes] = encode(value)
                else:
                    sent[s, way, h, q] = encode(part[q, s, :, block(o), :] + decode(got[s, way, h - 1, q]))
            red_copy(s, way, h).start()
            red_copy(s, way, h - 1).wait_send()

    def red_last(s):
        for way in range(2):
            red_copy(s, way, 3).wait_recv()
        gate, up, back = [
            part[q, s, :, block(z), :] + decode(got[s, 0, 3, q]) + decode(got[s, 1, 3, q]) for q in range(3)
        ]
        sig = 1.0 / (1.0 + jnp.exp(-gate))
        hid[0, s, :, block(z), :] = (gate * sig * up).astype(BF16)
        hid[1, s, :, block(z), :] = (back * up * sig * (1.0 + gate * (1.0 - sig))).astype(BF16)
        hid[2, s, :, block(z), :] = (back * gate * sig).astype(BF16)
        for way in range(2):
            gat_copy(s, way, 0, z).start()
        for way in range(2):
            red_copy(s, way, 3).wait_send()

    def gat_copy(s, way, a, o):
        if a == 3:
            ref = hid.at[:, s, :, block(o), pl.ds(*LANES[way])]
        else:
            ref = hid.at[:, s, :, block(o), :]
        return remote(ref, ref, gat_s.at[s, way, a], gat_r.at[s, way, a], side[way])

    def origin(way, a):
        return z + 8 - a if way == 0 else z + a

    def gat_hop(s, a):
        for way in range(2):
            gat_copy(s, way, a - 1, origin(way, a)).wait_recv()
            gat_copy(s, way, a, origin(way, a)).start()
        for way in range(2):
            gat_copy(s, way, a - 1, origin(way, a - 1)).wait_send()

    def gat_last(s):
        for way in range(2):
            gat_copy(s, way, 3, origin(way, 4)).wait_recv()
        for way in range(2):
            gat_copy(s, way, 3, origin(way, 3)).wait_send()

    def partials(s):
        tok = rows[0, s].reshape(256, 1024)
        part[0, s] = product(tok, wg_ref[...]).reshape(2, 128, 512)
        part[1, s] = product(tok, wu_ref[...]).reshape(2, 128, 512)
        cot = rows[1, s].reshape(256, 1024)
        part[2, s] = product(cot, wd_ref[...], INNER).reshape(2, 128, 512)

    def input_half(s, core):
        return product(hid[1, s, core], wg_ref[...], INNER) + product(hid[2, s, core], wu_ref[...], INNER)

    def give_copy(j):
        return remote(give.at[j], take.at[j], give_s.at[j], give_r.at[j], partner)

    def input_first(j, s):
        give[j] = input_half(s, 1 - c)
        give_copy(j).start()
        local[...] = input_half(s, c)

    def gi_copy(k, d):
        return remote(
            out16.at[k, d], in16.at[k, d], gi_s.at[k, d], gi_r.at[k, d], (at(x + k, y + d, c), z)
        )

    def input_second(j):
        give_copy(j).wait_recv()
        for d in range(4):
            place = pl.ds(pl.multiple_of(((y + d) % 4) * 32, 32), 32)
            value = (local[place, :] + take[j, place, :]).astype(BF16)

            if d == 0:

                @pl.when(j == 0)
                def _():
                    in16[0, 0] = value

                @pl.when(j > 0)
                def _():
                    out16[j, 0] = value
                    gi_copy(j, 0).start()
            else:
                out16[j, d] = value
                gi_copy(j, d).start()

    def weights(s, last):
        tok = rows.at[0, s]
        cot = rows[1, s].reshape(256, 1024)

        def tile(i, _):
            span = pl.ds(pl.multiple_of(i * 256, 256), 256)
            left = tok[:, :, span].reshape(256, 256)
            for q, out in ((1, gg_ref), (2, gu_ref)):
                value = acc[q - 1, span, :] + product(left, hid[q, s].reshape(256, 512), OUTER)
                if last:
                    out[span, :] = value.astype(BF16)
                else:
                    acc[q - 1, span, :] = value
            return 0

        lax.fori_loop(0, 4, tile, 0)

        def tile_down(i, _):
            span = pl.ds(pl.multiple_of(i * 256, 256), 256)
            left = hid[0, s, :, :, span].reshape(256, 256)
            value = accd[span, :] + product(left, cot, OUTER)
            if last:
                gd_ref[span, :] = value.astype(BF16)
            else:
                accd[span, :] = value
            return 0

        lax.fori_loop(0, 2, tile_down, 0)

    rows_send(0)
    rows_send(1)
    for a in range(2):
        rows[a, x, c, mine, :] = sources[a][...]
    acc[...] = jnp.zeros_like(acc)
    accd[...] = jnp.zeros_like(accd)

    def finish(j, s, last):
        gat_last(s)
        input_first(j, s)
        if not last:
            weights(s, False)
        input_second(j)
        if last:
            weights(s, True)

    def tick(t, _):
        for k in range(4):

            @pl.when(t == k)
            def _():
                rows_wait(k)
                if k + 2 < 4:
                    rows_send(k + 2)
                pair_send(k)

        for stage in range(8, -1, -1):
            j = t - stage
            s = (x + j + 8) % 4

            @pl.when((j >= 0) & (j < 4))
            def _():
                if stage == 0:
                    pair_wait(j)
                    partials(s)
                    red_first(s)
                elif stage < 4:
                    red_hop(s, stage)
                elif stage == 4:
                    red_last(s)
                elif stage < 8:
                    gat_hop(s, stage - 4)
                else:
                    finish(j, s, False)

        return 0

    lax.fori_loop(0, 11, tick, 0)
    finish(3, (x + 3) % 4, True)

    total = in16[0, 0].astype(F32)
    for k in range(4):
        for d in range(4):
            if (k, d) != (0, 0):
                gi_copy(k, d).wait_recv()
                total = total + in16[k, d].astype(F32)
    gi_ref[...] = total.astype(BF16)
    for k in range(4):
        give_copy(k).wait_send()
        for a in range(2):
            pair_copy(a, k, c).wait_send()
        for d in range(4):
            if (k, d) != (0, 0):
                gi_copy(k, d).wait_send()
                for a in range(2):
                    rows_copy(a, k, d).wait_send()


def body(tokens, cotangent, gate_weight, up_weight, down_weight):
    vmem = pl.BlockSpec(memory_space=pltpu.VMEM)
    dma = pltpu.SemaphoreType.DMA
    return pl.pallas_call(
        kernel,
        out_shape=(
            jax.ShapeDtypeStruct((1024, 512), BF16),
            jax.ShapeDtypeStruct((1024, 512), BF16),
            jax.ShapeDtypeStruct((512, 1024), BF16),
            jax.ShapeDtypeStruct((32, 1024), BF16),
        ),
        in_specs=[vmem] * 5,
        out_specs=(vmem,) * 4,
        scratch_shapes=[
            pltpu.VMEM((2, 4, 2, 128, 1024), BF16),
            pltpu.VMEM((3, 4, 2, 128, 512), F32),
            pltpu.VMEM((4, 2, 4, 3, 2, 16, 512), BF16),
            pltpu.VMEM((4, 2, 4, 3, 2, 16, 512), BF16),
            pltpu.VMEM((3, 4, 2, 128, 512), BF16),
            pltpu.VMEM((2, 1024, 512), F32),
            pltpu.VMEM((512, 1024), F32),
            pltpu.VMEM((4, 128, 1024), F32),
            pltpu.VMEM((4, 128, 1024), F32),
            pltpu.VMEM((4, 4, 32, 1024), BF16),
            pltpu.VMEM((4, 4, 32, 1024), BF16),
            pltpu.VMEM((128, 1024), F32),
            dma((2, 4, 4)), dma((2, 4, 4)),
            dma((2, 4)), dma((2, 4)),
            dma((4, 2, 4)), dma((4, 2, 4)),
            dma((4, 2, 4)), dma((4, 2, 4)),
            dma((4,)), dma((4,)),
            dma((4, 4)), dma((4, 4)),
        ],
        compiler_params=pltpu.CompilerParams(
            collective_id=0, has_side_effects=True, vmem_limit_bytes=56 * 2**20
        ),
    )(tokens, cotangent, gate_weight, up_weight, down_weight)


def solution(mesh):
    placed = (P("row", "col"), P("row", "col"), P("col", "row"), P("col", "row"), P("row", "col"))
    return jax.shard_map(
        body,
        mesh=mesh,
        in_specs=placed,
        out_specs=(P("col", "row"), P("col", "row"), P("row", "col"), P("row", "col")),
        check_vma=False,
    )
```

```python
import jax
import jax.numpy as jnp
from jax import lax
from jax.experimental import pallas as pl
from jax.experimental.pallas import tpu as pltpu
from jax.sharding import PartitionSpec as P

MESH = pl.DeviceIdType.MESH
F32, BF16 = jnp.float32, jnp.bfloat16
INNER = (((1,), (1,)), ((), ()))
OUTER = (((0,), (0,)), ((), ()))
SCALE = 2.0**51
WIDE = 1536
HALF = WIDE // 2
SLOTS = (
    (0, 0), (1, 0), (0, 1), (3, 0), (0, 3), (2, 0), (0, 2), (1, 1),
    (1, 3), (3, 1), (3, 3), (2, 1), (2, 3), (1, 2), (3, 2), (2, 2),
)
FIRST = ((0, 1, (3, 0)), (0, 2, (0, 3)), (0, 3, (1, 0)), (0, 4, (0, 1)), (0, 5, (2, 0)), (0, 6, (0, 2)))
SECOND = ((2, 7, (3, 0)), (1, 8, (0, 1)), (3, 9, (0, 3)), (4, 10, (1, 0)))
THIRD = ((7, 11, (3, 0)), (10, 12, (1, 0)), (7, 13, (0, 3)), (10, 14, (0, 1)))
FOURTH = ((13, 15, (3, 0)),)
ROUNDS = (FIRST, SECOND, THIRD, FOURTH)
ARRIVALS = ((1, 2, 3, 4), (5, 6, 7, 8, 9, 10), (11, 12, 13, 14), (15,))
ALL = FIRST + SECOND + THIRD + FOURTH


def encode(value):
    scaled = value * SCALE
    return (scaled * jnp.abs(scaled)).astype(BF16)


def decode(coded):
    wide = coded.astype(F32)
    return wide * lax.rsqrt(jnp.maximum(jnp.abs(wide), 1e-37)) * (1.0 / SCALE)


def product(a, b, dims=(((1,), (0,)), ((), ()))):
    return lax.dot_general(a, b, dims, preferred_element_type=F32)


def kernel(
    tok_ref, cot_ref, wg_ref, wu_ref, wd_ref,
    gg_ref, gu_ref, gd_ref, gi_ref,
    rows, both, down, part, sent, got, hid, acc, accd, give, take, out16, in16, local,
    load_s, rows_s, rows_r, pair_s, pair_r, red_s, red_r, gat_s, gat_r, give_s, give_r, gi_s, gi_r,
):
    row, z = lax.axis_index("row"), lax.axis_index("col")
    x, y, c = row // 8, (row // 2) % 4, row % 2

    def plane(offset):
        return (((x + offset[0]) % 4) * 4 + (y + offset[1]) % 4) * 2 + c, z

    partner = (row + 1 - 2 * c, z)
    side = ((row, (z + 1) % 8), (row, (z + 7) % 8))

    def remote(src, dst, s, r, device):
        return pltpu.make_async_remote_copy(
            src_ref=src, dst_ref=dst, send_sem=s, recv_sem=r, device_id=device, device_id_type=MESH
        )

    loads = [
        pltpu.make_async_copy(wg_ref, both.at[:, 0:512], load_s.at[0]),
        pltpu.make_async_copy(wu_ref, both.at[:, 512:1024], load_s.at[1]),
        pltpu.make_async_copy(wd_ref, down, load_s.at[2]),
    ]
    for load in loads:
        load.start()
    rows[0, 0, 0:32, :] = tok_ref[...]
    rows[1, 0, 0:32, :] = cot_ref[...]

    barrier = pltpu.get_barrier_semaphore()
    peers = [side[0], side[1], partner] + [plane(offset) for offset in SLOTS[1:]]
    for peer in peers:
        pl.semaphore_signal(barrier, inc=1, device_id=peer, device_id_type=MESH)
    pl.semaphore_wait(barrier, len(peers))

    def rows_copy(source, slot, offset):
        return remote(
            rows.at[:, source, 0:32], rows.at[:, slot, 0:32], rows_s.at[slot], rows_r.at[slot], plane(offset)
        )

    def pair_copy(slot, src, dst):
        return remote(
            rows.at[:, slot, src : src + 32], rows.at[:, slot, dst : dst + 32], pair_s.at[slot], pair_r.at[slot], partner
        )

    def rows_send(k):
        for send in ROUNDS[k]:
            rows_copy(*send).start()

    def rows_step(k):
        for slot in ARRIVALS[k]:
            rows_copy(slot, slot, SLOTS[slot]).wait_recv()
        if k < 3:
            rows_send(k + 1)
        for slot in ARRIVALS[k]:
            pair_copy(slot, 0, 32).start()

    def pair_wait(j):
        def wait(i, _):
            pair_copy(4 * j + i, 32, 32).wait_recv()
            return 0

        lax.fori_loop(0, 4, wait, 0)

    def block(o):
        return pl.ds(pl.multiple_of((o % 8) * 16, 16), 16)

    def lanes(way):
        return pl.ds(way * HALF, HALF)

    def red_copy(u, way, h):
        if h == 0:
            src, dst = sent.at[u, way, h, :, lanes(way)], got.at[u, way, h, :, lanes(way)]
        else:
            src, dst = sent.at[u, way, h], got.at[u, way, h]
        return remote(src, dst, red_s.at[u, way, h], red_r.at[u, way, h], side[way])

    def red_first(u):
        for way in range(2):
            sent[u, way, 0, :, lanes(way)] = encode(part[u, block(z + 4), lanes(way)])
            red_copy(u, way, 0).start()

    def red_hop(u, h):
        for way in range(2):
            o = z + 4 - h if way == 0 else z + 4 + h
            if h == 1:
                sent[u, way, h, :, lanes(1 - way)] = encode(part[u, block(o), lanes(1 - way)])
                red_copy(u, way, 0).wait_recv()
                value = part[u, block(o), lanes(way)] + decode(got[u, way, 0, :, lanes(way)])
                sent[u, way, h, :, lanes(way)] = encode(value)
            else:
                red_copy(u, way, h - 1).wait_recv()
                sent[u, way, h] = encode(part[u, block(o), :] + decode(got[u, way, h - 1]))
            red_copy(u, way, h).start()
        for way in range(2):
            red_copy(u, way, h - 1).wait_send()

    def red_last(u):
        for way in range(2):
            red_copy(u, way, 3).wait_recv()
        gate, up, back = [
            part[u, block(z), span] + decode(got[u, 0, 3, :, span]) + decode(got[u, 1, 3, :, span])
            for span in (pl.ds(0, 512), pl.ds(512, 512), pl.ds(1024, 512))
        ]
        sig = 1.0 / (1.0 + jnp.exp(-gate))
        hid[u, block(z), 0:512] = (back * up * sig * (1.0 + gate * (1.0 - sig))).astype(BF16)
        hid[u, block(z), 512:1024] = (back * gate * sig).astype(BF16)
        hid[u, block(z), 1024:1536] = (gate * sig * up).astype(BF16)
        for way in range(2):
            gat_copy(u, way, 0, z).start()
        for way in range(2):
            red_copy(u, way, 3).wait_send()

    def gat_copy(u, way, a, o):
        ref = hid.at[u, block(o), lanes(way)] if a == 3 else hid.at[u, block(o)]
        return remote(ref, ref, gat_s.at[u, way, a], gat_r.at[u, way, a], side[way])

    def origin(way, a):
        return z + 8 - a if way == 0 else z + a

    def gat_hop(u, a):
        for way in range(2):
            gat_copy(u, way, a - 1, origin(way, a)).wait_recv()
            gat_copy(u, way, a, origin(way, a)).start()
        for way in range(2):
            gat_copy(u, way, a - 1, origin(way, a - 1)).wait_send()

    def gat_last(u):
        for way in range(2):
            gat_copy(u, way, 3, origin(way, 4)).wait_recv()
        for way in range(2):
            gat_copy(u, way, 3, origin(way, 3)).wait_send()

    def units(j):
        return pl.ds(2 * j, 2)

    def slots(j):
        return pl.ds(4 * j, 4)

    def partials(j):
        tok = rows[0, slots(j)].reshape(256, 1024)
        cot = rows[1, slots(j)].reshape(256, 1024)
        part[units(j), :, 0:1024] = product(tok, both[...]).reshape(2, 128, 1024)
        part[units(j), :, 1024:1536] = product(cot, down[...], INNER).reshape(2, 128, 512)

    def give_copy(j):
        return remote(give.at[j], take.at[j], give_s.at[j], give_r.at[j], partner)

    def input_first(j):
        value = product(hid[units(j), :, 0:1024].reshape(256, 1024), both[...], INNER).reshape(4, 64, 1024)
        give[j] = value[:, 32:64]
        give_copy(j).start()
        local[...] = value[:, 0:32]

    def gi_copy(slot, offset):
        return remote(out16.at[slot], in16.at[slot], gi_s.at[slot], gi_r.at[slot], plane(offset))

    def input_second(j):
        give_copy(j).wait_recv()
        for k in range(4):

            @pl.when(j == k)
            def _():
                for i in range(4):
                    slot = 4 * k + i
                    value = (local[i] + take[k, i]).astype(BF16)
                    if slot == 0:
                        in16[0] = value
                    else:
                        out16[slot] = value
                        gi_copy(slot, SLOTS[slot]).start()

    def weights(j, last):
        cot = rows[1, slots(j)].reshape(256, 1024)

        def tile(i, _):
            span = pl.ds(pl.multiple_of(i * 256, 256), 256)
            left = rows[0, slots(j), :, span].reshape(256, 256)
            value = acc[span, :] + product(left, hid[units(j), :, 0:1024].reshape(256, 1024), OUTER)
            if last:
                gg_ref[span, :] = value[:, 0:512].astype(BF16)
                gu_ref[span, :] = value[:, 512:1024].astype(BF16)
            else:
                acc[span, :] = value
            return 0

        lax.fori_loop(0, 4, tile, 0)

        def tile_down(i, _):
            span = pl.ds(pl.multiple_of(i * 256, 256), 256)
            left = hid[units(j), :, pl.ds(pl.multiple_of(1024 + i * 256, 256), 256)].reshape(256, 256)
            value = accd[span, :] + product(left, cot, OUTER)
            if last:
                gd_ref[span, :] = value.astype(BF16)
            else:
                accd[span, :] = value
            return 0

        lax.fori_loop(0, 2, tile_down, 0)

    pair_copy(0, 0, 32).start()
    rows_send(0)
    acc[...] = jnp.zeros_like(acc)
    accd[...] = jnp.zeros_like(accd)
    for load in loads:
        load.wait()

    def each(j, step):
        for e in range(2):
            step(2 * j + e)

    def finish(j, last):
        each(j, gat_last)
        input_first(j)
        if not last:
            weights(j, False)
        input_second(j)
        if last:
            weights(j, True)

    def tick(t, _):
        for stage in range(8, -1, -1):
            j = t - stage

            @pl.when((j >= 0) & (j < 4))
            def _():
                if stage == 0:
                    for k in range(4):

                        @pl.when(j == k)
                        def _():
                            rows_step(k)

                    pair_wait(j)
                    partials(j)
                    each(j, red_first)
                elif stage < 4:
                    each(j, lambda u: red_hop(u, stage))
                elif stage == 4:
                    each(j, red_last)
                elif stage < 8:
                    each(j, lambda u: gat_hop(u, stage - 4))
                else:
                    finish(j, False)

        return 0

    lax.fori_loop(0, 11, tick, 0)
    finish(3, True)

    total = in16[0].astype(F32)
    for slot in range(1, 16):
        gi_copy(slot, SLOTS[slot]).wait_recv()
        total = total + in16[slot].astype(F32)
    gi_ref[...] = total.astype(BF16)
    for k in range(4):
        give_copy(k).wait_send()
    for slot in range(16):
        pair_copy(slot, 0, 32).wait_send()
    for slot in range(1, 16):
        gi_copy(slot, SLOTS[slot]).wait_send()
    for send in ALL:
        rows_copy(*send).wait_send()


def flush(gg_in, gu_in, gd_in, gi_in, gg_out, gu_out, gd_out, gi_out, sem):
    pairs = ((gg_in, gg_out), (gu_in, gu_out), (gd_in, gd_out), (gi_in, gi_out))
    copies = [pltpu.make_async_copy(src, dst, sem.at[i]) for i, (src, dst) in enumerate(pairs)]
    for copy in copies:
        copy.start()
    for copy in copies:
        copy.wait()


def body(tokens, cotangent, gate_weight, up_weight, down_weight):
    vmem = pl.BlockSpec(memory_space=pltpu.VMEM)
    hbm = pl.BlockSpec(memory_space=pl.ANY)
    dma = pltpu.SemaphoreType.DMA
    shapes = ((1024, 512), (1024, 512), (512, 1024), (32, 1024))
    results = pl.pallas_call(
        kernel,
        out_shape=tuple(pltpu.VMEM(shape, BF16) for shape in shapes),
        in_specs=[vmem] * 2 + [hbm] * 3,
        out_specs=(vmem,) * 4,
        scratch_shapes=[
            pltpu.VMEM((2, 16, 64, 1024), BF16),
            pltpu.VMEM((1024, 1024), BF16),
            pltpu.VMEM((512, 1024), BF16),
            pltpu.VMEM((8, 128, WIDE), F32),
            pltpu.VMEM((8, 2, 4, 16, WIDE), BF16),
            pltpu.VMEM((8, 2, 4, 16, WIDE), BF16),
            pltpu.VMEM((8, 128, WIDE), BF16),
            pltpu.VMEM((1024, 1024), F32),
            pltpu.VMEM((512, 1024), F32),
            pltpu.VMEM((4, 4, 32, 1024), F32),
            pltpu.VMEM((4, 4, 32, 1024), F32),
            pltpu.VMEM((16, 32, 1024), BF16),
            pltpu.VMEM((16, 32, 1024), BF16),
            pltpu.VMEM((4, 32, 1024), F32),
            dma((3,)),
            dma((16,)), dma((16,)),
            dma((16,)), dma((16,)),
            dma((8, 2, 4)), dma((8, 2, 4)),
            dma((8, 2, 4)), dma((8, 2, 4)),
            dma((4,)), dma((4,)),
            dma((16,)), dma((16,)),
        ],
        compiler_params=pltpu.CompilerParams(
            collective_id=0, has_side_effects=True, vmem_limit_bytes=56 * 2**20
        ),
    )(tokens, cotangent, gate_weight, up_weight, down_weight)
    return pl.pallas_call(
        flush,
        out_shape=tuple(jax.ShapeDtypeStruct(shape, BF16) for shape in shapes),
        in_specs=[vmem] * 4,
        out_specs=(hbm,) * 4,
        scratch_shapes=[dma((4,))],
        compiler_params=pltpu.CompilerParams(vmem_limit_bytes=8 * 2**20),
    )(*results)


def solution(mesh):
    placed = (P("row", "col"), P("row", "col"), P("col", "row"), P("col", "row"), P("row", "col"))
    return jax.shard_map(
        body,
        mesh=mesh,
        in_specs=placed,
        out_specs=(P("col", "row"), P("col", "row"), P("row", "col"), P("row", "col")),
        check_vma=False,
    )
```

```python
import jax
import jax.numpy as jnp
from jax import lax
from jax.experimental import pallas as pl
from jax.experimental.pallas import tpu as pltpu
from jax.sharding import PartitionSpec as P

MESH = pl.DeviceIdType.MESH
F32, BF16 = jnp.float32, jnp.bfloat16
INNER = (((1,), (1,)), ((), ()))
OUTER = (((0,), (0,)), ((), ()))
SCALE = 2.0**51
WIDE = 1536
HALF = WIDE // 2
OWN = (0, 0)
SLOTS = (
    (0, 3), (1, 1), (1, 3), (3, 1), (3, 3), (2, 0), (0, 2), (2, 1),
    (2, 3), (1, 2), (3, 2), (2, 2), (0, 0), (1, 0), (0, 1), (3, 0),
)
PLACE = {offset: slot for slot, offset in enumerate(SLOTS)}
FIRST = tuple((OWN, to, 0, 32) for to in ((3, 0), (1, 0), (0, 3), (0, 1)))
SECOND = (
    ((0, 1), (3, 0), 0, 32), ((0, 3), (1, 0), 0, 32), ((1, 0), (0, 1), 0, 32), ((3, 0), (0, 3), 0, 32),
    ((1, 0), (3, 0), 0, 16), ((3, 0), (1, 0), 16, 16), ((0, 1), (0, 3), 0, 16), ((0, 3), (0, 1), 16, 16),
)
THIRD = (
    ((1, 1), (3, 0), 0, 32), ((3, 3), (1, 0), 0, 32), ((1, 1), (0, 3), 0, 32), ((3, 3), (0, 1), 0, 32),
    (OWN, (2, 2), 0, 32),
)
ROUNDS = (FIRST, SECOND, THIRD)
ARRIVALS = (
    ((1, 0), (3, 0), (0, 1), (0, 3)),
    ((1, 1), (1, 3), (3, 1), (3, 3)),
    ((2, 0), (0, 2)),
    ((2, 1), (2, 3), (1, 2), (3, 2)),
    ((2, 2),),
)
ROWS, PART, RED0, RED1, RED2, RED3, RED4, GAT1, GAT2, GAT3, GAT4, GIVE, SEND, PAST = range(14)
ORDER = (
    (ROWS, 0), (PART, 6), (RED0, 6), (PART, 7), (RED0, 7), (RED1, 6), (ROWS, 1), (RED1, 7),
    (ROWS, 2), (PART, 0), (RED0, 0), (PART, 1), (RED0, 1), (PART, 2), (RED0, 2), (RED2, 6),
    (RED2, 7), (RED1, 0), (ROWS, 3), (RED1, 1), (RED1, 2), (PART, 3), (ROWS, 4), (RED0, 3),
    (RED3, 6), (PART, 4), (RED0, 4), (RED3, 7), (PART, 5), (RED0, 5), (RED2, 0), (RED2, 1),
    (RED2, 2), (RED1, 3), (RED1, 4), (RED1, 5), (RED3, 0), (RED3, 1), (RED3, 2), (RED2, 3),
    (RED2, 4), (RED2, 5), (RED4, 0), (RED4, 1), (RED4, 2), (RED3, 3), (RED3, 4), (RED3, 5),
    (GAT1, 0), (GAT1, 1), (GAT1, 2), (RED4, 3), (RED4, 4), (RED4, 5), (RED4, 6), (GAT2, 0),
    (GAT2, 1), (GAT2, 2), (GAT1, 3), (GAT1, 4), (RED4, 7), (GAT1, 5), (GAT1, 6), (GAT3, 0),
    (GAT3, 1), (GAT3, 2), (GAT2, 3), (GAT2, 4), (GAT1, 7), (GAT2, 5), (GAT2, 6), (GAT4, 0),
    (GIVE, 0), (GAT4, 1), (GIVE, 1), (GAT4, 2), (GIVE, 2), (GAT3, 3), (SEND, 0), (GAT3, 4),
    (SEND, 1), (SEND, 2), (GAT2, 7), (GAT3, 5), (GAT3, 6), (GAT4, 3), (GIVE, 3), (GAT4, 4),
    (GIVE, 4), (GAT3, 7), (PAST, 0), (GAT4, 5), (GIVE, 5), (GAT4, 6), (SEND, 3), (SEND, 4),
    (GIVE, 6), (PAST, 1), (GAT4, 7), (SEND, 5), (GIVE, 7), (PAST, 2), (SEND, 6), (PAST, 3),
    (PAST, 4), (SEND, 7), (PAST, 5),
)


def encode(value):
    scaled = value * SCALE
    return (scaled * jnp.abs(scaled)).astype(BF16)


def decode(coded):
    wide = coded.astype(F32)
    return wide * lax.rsqrt(jnp.maximum(jnp.abs(wide), 1e-37)) * (1.0 / SCALE)


def product(a, b, dims=(((1,), (0,)), ((), ()))):
    return lax.dot_general(a, b, dims, preferred_element_type=F32)


def kernel(
    tok_ref, cot_ref, wg_ref, wu_ref, wd_ref,
    gg_ref, gu_ref, gd_ref, gi_ref,
    rows, both, down, part, sent, got, hid, acc, accd, give, take, out16, in16, local,
    load_s, rows_s, rows_r, pair_s, pair_r, red_s, red_r, gat_s, gat_r, give_s, give_r, gi_s, gi_r,
):
    row, z = lax.axis_index("row"), lax.axis_index("col")
    x, y, c = row // 8, (row // 2) % 4, row % 2

    def plane(offset):
        return (((x + offset[0]) % 4) * 4 + (y + offset[1]) % 4) * 2 + c, z

    partner = (row + 1 - 2 * c, z)
    side = ((row, (z + 1) % 8), (row, (z + 7) % 8))

    def remote(src, dst, s, r, device):
        return pltpu.make_async_remote_copy(
            src_ref=src, dst_ref=dst, send_sem=s, recv_sem=r, device_id=device, device_id_type=MESH
        )

    barrier = pltpu.get_barrier_semaphore()
    peers = [side[0], side[1], partner] + [plane(offset) for offset in SLOTS if offset != OWN]
    for peer in peers:
        pl.semaphore_signal(barrier, inc=1, device_id=peer, device_id_type=MESH)
    own = PLACE[OWN]
    loads = [
        pltpu.make_async_copy(tok_ref, rows.at[0, own, 0:32], load_s.at[0]),
        pltpu.make_async_copy(cot_ref, rows.at[1, own, 0:32], load_s.at[1]),
        pltpu.make_async_copy(wg_ref, both.at[:, 0:512], load_s.at[2]),
        pltpu.make_async_copy(wu_ref, both.at[:, 512:1024], load_s.at[3]),
        pltpu.make_async_copy(wd_ref, down, load_s.at[4]),
    ]
    for load in loads:
        load.start()
    for load in loads[:2]:
        load.wait()
    pl.semaphore_wait(barrier, len(peers))

    def rows_copy(source, to, first, count):
        lands = PLACE[((source[0] - to[0]) % 4, (source[1] - to[1]) % 4)]
        sem = lands if first == 0 else 16 + (PLACE[(0, 2)] == lands)
        return remote(
            rows.at[:, PLACE[source], first : first + count],
            rows.at[:, lands, first : first + count],
            rows_s.at[sem],
            rows_r.at[sem],
            plane(to),
        )

    def pair_copy(slot, src, dst):
        return remote(
            rows.at[:, slot, src : src + 32], rows.at[:, slot, dst : dst + 32], pair_s.at[slot], pair_r.at[slot], partner
        )

    def rows_send(k):
        for send in ROUNDS[k]:
            rows_copy(*send).start()

    def rows_step(k):
        for send in (send for sends in ROUNDS for send in sends):
            source, to, first, count = send
            offset = ((source[0] - to[0]) % 4, (source[1] - to[1]) % 4)
            if offset in ARRIVALS[k]:
                ref = rows.at[:, PLACE[offset], first : first + count]
                sem = PLACE[offset] if first == 0 else 16 + (offset == (0, 2))
                remote(ref, ref, rows_s.at[sem], rows_r.at[sem], partner).wait_recv()
        if k < 2:
            rows_send(k + 1)
        for offset in ARRIVALS[k]:
            pair_copy(PLACE[offset], 0, 32).start()

    def partials(u):
        for slot in (2 * u, 2 * u + 1):
            pair_copy(slot, 32, 32).wait_recv()
        tok = rows[0, 2 * u : 2 * u + 2].reshape(128, 1024)
        cot = rows[1, 2 * u : 2 * u + 2].reshape(128, 1024)
        part[u, :, 0:1024] = product(tok, both[...])
        part[u, :, 1024:1536] = product(cot, down[...], INNER)

    def block(o):
        return pl.ds(pl.multiple_of((o % 8) * 16, 16), 16)

    def lanes(way):
        return pl.ds(way * HALF, HALF)

    def red_copy(u, way, h):
        if h == 0:
            src, dst = sent.at[u, way, h, :, lanes(way)], got.at[u, way, h, :, lanes(way)]
        else:
            src, dst = sent.at[u, way, h], got.at[u, way, h]
        return remote(src, dst, red_s.at[u, way, h], red_r.at[u, way, h], side[way])

    def red_first(u):
        for way in range(2):
            sent[u, way, 0, :, lanes(way)] = encode(part[u, block(z + 4), lanes(way)])
            red_copy(u, way, 0).start()

    def red_hop(u, h):
        for way in range(2):
            o = z + 4 - h if way == 0 else z + 4 + h
            if h == 1:
                sent[u, way, h, :, lanes(1 - way)] = encode(part[u, block(o), lanes(1 - way)])
                red_copy(u, way, 0).wait_recv()
                value = part[u, block(o), lanes(way)] + decode(got[u, way, 0, :, lanes(way)])
                sent[u, way, h, :, lanes(way)] = encode(value)
            else:
                red_copy(u, way, h - 1).wait_recv()
                sent[u, way, h] = encode(part[u, block(o), :] + decode(got[u, way, h - 1]))
            red_copy(u, way, h).start()
        for way in range(2):
            red_copy(u, way, h - 1).wait_send()

    def red_last(u):
        for way in range(2):
            red_copy(u, way, 3).wait_recv()
        gate, up, back = [
            part[u, block(z), span] + decode(got[u, 0, 3, :, span]) + decode(got[u, 1, 3, :, span])
            for span in (pl.ds(0, 512), pl.ds(512, 512), pl.ds(1024, 512))
        ]
        sig = 1.0 / (1.0 + jnp.exp(-gate))
        hid[u, block(z), 0:512] = (back * up * sig * (1.0 + gate * (1.0 - sig))).astype(BF16)
        hid[u, block(z), 512:1024] = (back * gate * sig).astype(BF16)
        hid[u, block(z), 1024:1536] = (gate * sig * up).astype(BF16)
        for way in range(2):
            gat_copy(u, way, 0, z).start()
        for way in range(2):
            red_copy(u, way, 3).wait_send()

    def gat_copy(u, way, a, o):
        ref = hid.at[u, block(o), lanes(way)] if a == 3 else hid.at[u, block(o)]
        return remote(ref, ref, gat_s.at[u, way, a], gat_r.at[u, way, a], side[way])

    def origin(way, a):
        return z + 8 - a if way == 0 else z + a

    def gat_hop(u, a):
        for way in range(2):
            gat_copy(u, way, a - 1, origin(way, a)).wait_recv()
            gat_copy(u, way, a, origin(way, a)).start()
        for way in range(2):
            gat_copy(u, way, a - 1, origin(way, a - 1)).wait_send()

    def gat_last(u):
        for way in range(2):
            gat_copy(u, way, 3, origin(way, 4)).wait_recv()
        for way in range(2):
            gat_copy(u, way, 3, origin(way, 3)).wait_send()

    def give_copy(u):
        return remote(give.at[u], take.at[u], give_s.at[u], give_r.at[u], partner)

    def input_first(u):
        value = product(hid[u, :, 0:1024], both[...], INNER).reshape(2, 64, 1024)
        give[u] = value[:, 32:64]
        give_copy(u).start()
        local[u] = value[:, 0:32]

    def gi_copy(slot):
        return remote(out16.at[slot], in16.at[slot], gi_s.at[slot], gi_r.at[slot], plane(SLOTS[slot]))

    def input_second(u):
        give_copy(u).wait_recv()
        for i in range(2):
            slot = 2 * u + i
            value = (local[u, i] + take[u, i]).astype(BF16)
            if slot == own:
                in16[slot] = value
            else:
                out16[slot] = value
                gi_copy(slot).start()

    def weights(i, half):
        span = pl.ds((i % 4) * 256, 256)
        if i < 4:
            left = rows[0, 8 * half : 8 * half + 8, :, span].reshape(512, 256)
            value = product(left, hid[4 * half : 4 * half + 4, :, 0:1024].reshape(512, 1024), OUTER)
            if half == 0:
                acc[span, :] = value
            else:
                value = acc[span, :] + value
                gg_ref[span, :] = value[:, 0:512].astype(BF16)
                gu_ref[span, :] = value[:, 512:1024].astype(BF16)
        else:
            left = hid[4 * half : 4 * half + 4, :, pl.ds(1024 + (i % 4) * 256, 256)].reshape(512, 256)
            value = product(left, rows[1, 8 * half : 8 * half + 8].reshape(512, 1024), OUTER)
            if half == 0:
                accd[span, :] = value
            else:
                gd_ref[span, :] = (accd[span, :] + value).astype(BF16)

    pair_copy(own, 0, 32).start()
    rows_send(0)
    for load in loads[2:]:
        load.wait()
    for step, n in ORDER:
        if step == ROWS:
            rows_step(n)
        elif step == PART:
            partials(n)
        elif step == RED0:
            red_first(n)
        elif step < RED4:
            red_hop(n, step - RED0)
        elif step == RED4:
            red_last(n)
        elif step < GAT4:
            gat_hop(n, step - GAT1 + 1)
        elif step == GAT4:
            gat_last(n)
        elif step == GIVE:
            input_first(n)
        elif step == SEND:
            input_second(n)
        else:
            weights(n, 0)
    for i in range(6):
        weights(i, 1)

    for u in range(8):
        give_copy(u).wait_send()
    for slot in range(16):
        pair_copy(slot, 0, 32).wait_send()
    for sends in ROUNDS:
        for send in sends:
            rows_copy(*send).wait_send()
    total = in16[own].astype(F32)
    for slot in range(16):
        if slot != own:
            gi_copy(slot).wait_send()
            gi_copy(slot).wait_recv()
            total = total + in16[slot].astype(F32)
    gi_ref[...] = total.astype(BF16)


def flush(gg_in, gu_in, gd_in, gi_in, gg_out, gu_out, gd_out, gi_out, sem):
    pairs = ((gg_in, gg_out), (gu_in, gu_out), (gd_in, gd_out), (gi_in, gi_out))
    copies = [pltpu.make_async_copy(src, dst, sem.at[i]) for i, (src, dst) in enumerate(pairs)]
    for copy in copies:
        copy.start()
    for copy in copies:
        copy.wait()


def body(tokens, cotangent, gate_weight, up_weight, down_weight):
    vmem = pl.BlockSpec(memory_space=pltpu.VMEM)
    hbm = pl.BlockSpec(memory_space=pl.ANY)
    dma = pltpu.SemaphoreType.DMA
    shapes = ((1024, 512), (1024, 512), (512, 1024), (32, 1024))
    results = pl.pallas_call(
        kernel,
        out_shape=tuple(pltpu.VMEM(shape, BF16) for shape in shapes),
        in_specs=[hbm] * 5,
        out_specs=(vmem,) * 4,
        scratch_shapes=[
            pltpu.VMEM((2, 16, 64, 1024), BF16),
            pltpu.VMEM((1024, 1024), BF16),
            pltpu.VMEM((512, 1024), BF16),
            pltpu.VMEM((8, 128, WIDE), F32),
            pltpu.VMEM((8, 2, 4, 16, WIDE), BF16),
            pltpu.VMEM((8, 2, 4, 16, WIDE), BF16),
            pltpu.VMEM((8, 128, WIDE), BF16),
            pltpu.VMEM((1024, 1024), F32),
            pltpu.VMEM((512, 1024), F32),
            pltpu.VMEM((8, 2, 32, 1024), F32),
            pltpu.VMEM((8, 2, 32, 1024), F32),
            pltpu.VMEM((16, 32, 1024), BF16),
            pltpu.VMEM((16, 32, 1024), BF16),
            pltpu.VMEM((8, 2, 32, 1024), F32),
            dma((5,)),
            dma((18,)), dma((18,)),
            dma((16,)), dma((16,)),
            dma((8, 2, 4)), dma((8, 2, 4)),
            dma((8, 2, 4)), dma((8, 2, 4)),
            dma((8,)), dma((8,)),
            dma((16,)), dma((16,)),
        ],
        compiler_params=pltpu.CompilerParams(
            collective_id=0, has_side_effects=True, vmem_limit_bytes=56 * 2**20
        ),
    )(tokens, cotangent, gate_weight, up_weight, down_weight)
    return pl.pallas_call(
        flush,
        out_shape=tuple(jax.ShapeDtypeStruct(shape, BF16) for shape in shapes),
        in_specs=[vmem] * 4,
        out_specs=(hbm,) * 4,
        scratch_shapes=[dma((4,))],
        compiler_params=pltpu.CompilerParams(vmem_limit_bytes=8 * 2**20),
    )(*results)


def solution(mesh):
    placed = (P("row", "col"), P("row", "col"), P("col", "row"), P("col", "row"), P("row", "col"))
    return jax.shard_map(
        body,
        mesh=mesh,
        in_specs=placed,
        out_specs=(P("col", "row"), P("col", "row"), P("row", "col"), P("row", "col")),
        check_vma=False,
    )
```

```python
import jax
import jax.numpy as jnp
from jax import lax
from jax.experimental import pallas as pl
from jax.experimental.pallas import tpu as pltpu
from jax.sharding import PartitionSpec as P

MESH = pl.DeviceIdType.MESH
F32, BF16 = jnp.float32, jnp.bfloat16
INNER = (((1,), (1,)), ((), ()))
OUTER = (((0,), (0,)), ((), ()))
SCALE = 2.0**51
WIDE, HALF = 1536, 768
OWN = (0, 0)
SLOTS = (
    (0, 0), (1, 0), (0, 1), (3, 0), (0, 3), (1, 1), (1, 3), (3, 1),
    (3, 3), (2, 0), (0, 2), (2, 1), (2, 3), (1, 2), (3, 2), (2, 2),
)
PLACE = {offset: slot for slot, offset in enumerate(SLOTS)}
FIRST = tuple((OWN, to, 0, 32) for to in ((3, 0), (1, 0), (0, 3), (0, 1)))
SECOND = (
    ((0, 1), (3, 0), 0, 32), ((0, 3), (1, 0), 0, 32), ((1, 0), (0, 1), 0, 32), ((3, 0), (0, 3), 0, 32),
    ((1, 0), (3, 0), 0, 16), ((3, 0), (1, 0), 16, 16), ((0, 1), (0, 3), 0, 16), ((0, 3), (0, 1), 16, 16),
)
THIRD = (
    ((1, 1), (3, 0), 0, 32), ((3, 3), (1, 0), 0, 32), ((1, 1), (0, 3), 0, 32), ((3, 3), (0, 1), 0, 32),
    (OWN, (2, 2), 0, 32),
)
ROUNDS = (FIRST, SECOND, THIRD)
ARRIVALS = (
    ((1, 0), (3, 0), (0, 1), (0, 3)),
    ((1, 1), (1, 3), (3, 1), (3, 3)),
    ((2, 0), (0, 2)),
    ((2, 1), (2, 3), (1, 2), (3, 2)),
    ((2, 2),),
)
ROWS, PART, RED0, RED1, RED2, RED3, RED4, GAT1, GAT2, GAT3, GAT4, GIVE, SEND = range(13)
HID0, HID1, HID2, HID3, HID4, PAST, DOWN, LAST = range(13, 21)
ORDER = (
    (ROWS, 0), (PART, 0), (RED0, 0), (PART, 1), (RED0, 1), (RED1, 0), (ROWS, 1), (RED1, 1),
    (ROWS, 2), (PART, 2), (RED0, 2), (PART, 3), (RED0, 3), (PART, 4), (RED2, 0), (RED0, 4),
    (RED2, 1), (RED1, 2), (ROWS, 3), (RED1, 3), (PART, 5), (ROWS, 4), (RED3, 0), (RED0, 5),
    (RED1, 4), (PART, 6), (RED3, 1), (RED0, 6), (PART, 7), (RED2, 2), (RED0, 7), (RED2, 3),
    (RED4, 0), (RED1, 5), (RED2, 4), (RED4, 1), (RED1, 6), (RED3, 2), (RED1, 7), (RED3, 3),
    (GAT1, 0), (RED2, 5), (RED3, 4), (GAT1, 1), (RED2, 6), (RED4, 2), (RED2, 7), (RED4, 3),
    (GAT2, 0), (RED3, 5), (RED4, 4), (GAT2, 1), (RED3, 6), (GAT1, 2), (RED3, 7), (GAT1, 3),
    (GAT3, 0), (RED4, 5), (GAT1, 4), (GAT3, 1), (RED4, 6), (GAT2, 2), (RED4, 7), (GAT2, 3),
    (GAT4, 0), (GIVE, 0), (GAT1, 5), (GAT2, 4), (GAT4, 1), (GIVE, 1), (GAT1, 6), (SEND, 0),
    (GAT3, 2), (GAT1, 7), (SEND, 1), (GAT3, 3), (GAT2, 5), (GAT3, 4), (GAT2, 6), (GAT4, 2),
    (GIVE, 2), (GAT2, 7), (GAT4, 3), (GIVE, 3), (GAT3, 5), (HID0, 0), (PAST, 0), (GAT4, 4),
    (SEND, 2), (GAT3, 6), (HID0, 1), (GIVE, 4), (SEND, 3), (GAT3, 7), (PAST, 1), (PAST, 2),
    (GAT4, 5), (GIVE, 5), (SEND, 4), (HID1, 0), (PAST, 3), (GAT4, 6), (GIVE, 6), (SEND, 5),
    (HID1, 1), (GAT4, 7), (GIVE, 7), (PAST, 4), (SEND, 6), (PAST, 5), (HID2, 0), (PAST, 6),
    (SEND, 7), (PAST, 7), (HID2, 1), (HID3, 0), (HID3, 1), (HID4, 0), (DOWN, 0), (DOWN, 1),
    (LAST, 0), (HID4, 1), (DOWN, 2), (DOWN, 3),
)


def encode(value):
    scaled = value * SCALE
    return (scaled * jnp.abs(scaled)).astype(BF16)


def decode(coded):
    wide = coded.astype(F32)
    return wide * lax.rsqrt(jnp.maximum(jnp.abs(wide), 1e-37)) * (1.0 / SCALE)


def product(a, b, dims=(((1,), (0,)), ((), ()))):
    return lax.dot_general(a, b, dims, preferred_element_type=F32)


def kernel(
    tok_ref, cot_ref, wg_ref, wu_ref, wd_ref,
    gg_ref, gu_ref, gd_ref, gi_ref,
    rows, both, down, part, sent, got, hid, hidden, acc, accd, give, take, out16, in16, local,
    load_s, rows_s, rows_r, pair_s, pair_r, red_s, red_r, gat_s, gat_r, hid_s, hid_r, give_s, give_r, gi_s, gi_r,
):
    row, z = lax.axis_index("row"), lax.axis_index("col")
    x, y, c = row // 8, (row // 2) % 4, row % 2

    def plane(offset):
        return (((x + offset[0]) % 4) * 4 + (y + offset[1]) % 4) * 2 + c, z

    partner = (row + 1 - 2 * c, z)
    side = ((row, (z + 1) % 8), (row, (z + 7) % 8))

    def remote(src, dst, s, r, device):
        return pltpu.make_async_remote_copy(
            src_ref=src, dst_ref=dst, send_sem=s, recv_sem=r, device_id=device, device_id_type=MESH
        )

    barrier = pltpu.get_barrier_semaphore()
    peers = [side[0], side[1], partner] + [plane(offset) for offset in SLOTS if offset != OWN]
    for peer in peers:
        pl.semaphore_signal(barrier, inc=1, device_id=peer, device_id_type=MESH)
    own = PLACE[OWN]
    loads = [
        pltpu.make_async_copy(tok_ref, rows.at[0, own, 0:32], load_s.at[0]),
        pltpu.make_async_copy(cot_ref, rows.at[1, own, 0:32], load_s.at[1]),
        pltpu.make_async_copy(wg_ref, both.at[:, 0:512], load_s.at[2]),
        pltpu.make_async_copy(wu_ref, both.at[:, 512:1024], load_s.at[3]),
        pltpu.make_async_copy(wd_ref, down, load_s.at[4]),
    ]
    for load in loads:
        load.start()
    for load in loads[:2]:
        load.wait()
    pl.semaphore_wait(barrier, len(peers))

    def rows_copy(source, to, first, count):
        lands = PLACE[((source[0] - to[0]) % 4, (source[1] - to[1]) % 4)]
        sem = lands if first == 0 else 16 + (PLACE[(0, 2)] == lands)
        return remote(
            rows.at[:, PLACE[source], first : first + count],
            rows.at[:, lands, first : first + count],
            rows_s.at[sem],
            rows_r.at[sem],
            plane(to),
        )

    def pair_copy(slot, src, dst):
        return remote(
            rows.at[:, slot, src : src + 32], rows.at[:, slot, dst : dst + 32], pair_s.at[slot], pair_r.at[slot], partner
        )

    def rows_send(k):
        for send in ROUNDS[k]:
            rows_copy(*send).start()

    def rows_step(k):
        for send in (send for sends in ROUNDS for send in sends):
            source, to, first, count = send
            offset = ((source[0] - to[0]) % 4, (source[1] - to[1]) % 4)
            if offset in ARRIVALS[k]:
                ref = rows.at[:, PLACE[offset], first : first + count]
                sem = PLACE[offset] if first == 0 else 16 + (offset == (0, 2))
                remote(ref, ref, rows_s.at[sem], rows_r.at[sem], partner).wait_recv()
        if k < 2:
            rows_send(k + 1)
        for offset in ARRIVALS[k]:
            pair_copy(PLACE[offset], 0, 32).start()

    def partials(u):
        for slot in (2 * u, 2 * u + 1):
            pair_copy(slot, 32, 32).wait_recv()
        tok = rows[0, 2 * u : 2 * u + 2].reshape(128, 1024)
        cot = rows[1, 2 * u : 2 * u + 2].reshape(128, 1024)
        part[u, :, 0:1024] = product(tok, both[...])
        part[u, :, 1024:1536] = product(cot, down[...], INNER)

    def block(o):
        return pl.ds(pl.multiple_of((o % 8) * 16, 16), 16)

    def lanes(way):
        return pl.ds(way * HALF, HALF)

    def red_copy(u, way, h):
        if h == 0:
            src, dst = sent.at[u, way, h, :, lanes(way)], got.at[u, way, h, :, lanes(way)]
        else:
            src, dst = sent.at[u, way, h], got.at[u, way, h]
        return remote(src, dst, red_s.at[u, way, h], red_r.at[u, way, h], side[way])

    def red_first(u):
        for way in range(2):
            sent[u, way, 0, :, lanes(way)] = encode(part[u, block(z + 4), lanes(way)])
            red_copy(u, way, 0).start()

    def red_hop(u, h):
        for way in range(2):
            o = z + 4 - h if way == 0 else z + 4 + h
            if h == 1:
                sent[u, way, h, :, lanes(1 - way)] = encode(part[u, block(o), lanes(1 - way)])
                red_copy(u, way, 0).wait_recv()
                value = part[u, block(o), lanes(way)] + decode(got[u, way, 0, :, lanes(way)])
                sent[u, way, h, :, lanes(way)] = encode(value)
            else:
                red_copy(u, way, h - 1).wait_recv()
                sent[u, way, h] = encode(part[u, block(o), :] + decode(got[u, way, h - 1]))
            red_copy(u, way, h).start()
        for way in range(2):
            red_copy(u, way, h - 1).wait_send()

    def red_last(u):
        for way in range(2):
            red_copy(u, way, 3).wait_recv()
        gate, up, back = [
            part[u, block(z), span] + decode(got[u, 0, 3, :, span]) + decode(got[u, 1, 3, :, span])
            for span in (pl.ds(0, 512), pl.ds(512, 512), pl.ds(1024, 512))
        ]
        sig = 1.0 / (1.0 + jnp.exp(-gate))
        hid[u, block(z), 0:512] = (back * up * sig * (1.0 + gate * (1.0 - sig))).astype(BF16)
        hid[u, block(z), 512:1024] = (back * gate * sig).astype(BF16)
        hidden[u, block(z), :] = (gate * sig * up).astype(BF16)
        for way in range(2):
            gat_copy(u, way, 0, z).start()
        for way in range(2):
            red_copy(u, way, 3).wait_send()

    def gat_copy(u, way, a, o):
        ref = hid.at[u, block(o), pl.ds(way * 512, 512)] if a == 3 else hid.at[u, block(o)]
        return remote(ref, ref, gat_s.at[u, way, a], gat_r.at[u, way, a], side[way])

    def origin(way, a):
        return z + 8 - a if way == 0 else z + a

    def gat_hop(u, a):
        for way in range(2):
            gat_copy(u, way, a - 1, origin(way, a)).wait_recv()
            gat_copy(u, way, a, origin(way, a)).start()
        for way in range(2):
            gat_copy(u, way, a - 1, origin(way, a - 1)).wait_send()

    def gat_last(u):
        for way in range(2):
            gat_copy(u, way, 3, origin(way, 4)).wait_recv()
        for way in range(2):
            gat_copy(u, way, 3, origin(way, 3)).wait_send()

    def hid_copy(g, way, a, o):
        span = pl.ds(way * 256, 256) if a == 3 else pl.ds(0, 512)
        ref = hidden.at[4 * g : 4 * g + 4, block(o), span]
        return remote(ref, ref, hid_s.at[g, way, a], hid_r.at[g, way, a], side[way])

    def hid_hop(g, a):
        for way in range(2):
            if a > 0:
                hid_copy(g, way, a - 1, origin(way, a)).wait_recv()
            if a < 4:
                hid_copy(g, way, a, origin(way, a)).start()
        if a > 0:
            for way in range(2):
                hid_copy(g, way, a - 1, origin(way, a - 1)).wait_send()

    def give_copy(u):
        return remote(give.at[u], take.at[u], give_s.at[u], give_r.at[u], partner)

    def input_first(u):
        value = product(hid[u], both[...], INNER).reshape(2, 64, 1024)
        give[u] = value[:, 32:64]
        give_copy(u).start()
        local[u] = value[:, 0:32]

    def gi_copy(slot):
        return remote(out16.at[slot], in16.at[slot], gi_s.at[slot], gi_r.at[slot], plane(SLOTS[slot]))

    def input_second(u):
        give_copy(u).wait_recv()
        for i in range(2):
            slot = 2 * u + i
            value = (local[u, i] + take[u, i]).astype(BF16)
            if slot == own:
                in16[slot] = value
            else:
                out16[slot] = value
                gi_copy(slot).start()

    def input_last():
        total = in16[own].astype(F32)
        for slot in range(16):
            if slot != own:
                gi_copy(slot).wait_recv()
                total = total + in16[slot].astype(F32)
        gi_ref[...] = total.astype(BF16)

    def weights(i, half):
        span = pl.ds(i * 256, 256)
        left = rows[0, 8 * half : 8 * half + 8, :, span].reshape(512, 256)
        value = product(left, hid[4 * half : 4 * half + 4].reshape(512, 1024), OUTER)
        if half == 0:
            acc[span, :] = value
        else:
            value = acc[span, :] + value
            gg_ref[span, :] = value[:, 0:512].astype(BF16)
            gu_ref[span, :] = value[:, 512:1024].astype(BF16)

    def weights_down(i, half):
        span = pl.ds(i * 256, 256)
        left = hidden[4 * half : 4 * half + 4, :, span].reshape(512, 256)
        value = product(left, rows[1, 8 * half : 8 * half + 8].reshape(512, 1024), OUTER)
        if half == 0:
            accd[span, :] = value
        else:
            gd_ref[span, :] = (accd[span, :] + value).astype(BF16)

    pair_copy(own, 0, 32).start()
    rows_send(0)
    for load in loads[2:]:
        load.wait()
    for step, n in ORDER:
        if step == ROWS:
            rows_step(n)
        elif step == PART:
            partials(n)
        elif step == RED0:
            red_first(n)
        elif step < RED4:
            red_hop(n, step - RED0)
        elif step == RED4:
            red_last(n)
        elif step < GAT4:
            gat_hop(n, step - GAT1 + 1)
        elif step == GAT4:
            gat_last(n)
        elif step == GIVE:
            input_first(n)
        elif step == SEND:
            input_second(n)
        elif step == LAST:
            input_last()
        elif step < PAST:
            hid_hop(n, step - HID0)
        elif step == PAST:
            weights(n % 4, n // 4)
        else:
            weights_down(n % 2, n // 2)

    for u in range(8):
        give_copy(u).wait_send()
    for slot in range(16):
        pair_copy(slot, 0, 32).wait_send()
        if slot != own:
            gi_copy(slot).wait_send()
    for sends in ROUNDS:
        for send in sends:
            rows_copy(*send).wait_send()


def flush(gg_in, gu_in, gd_in, gi_in, gg_out, gu_out, gd_out, gi_out, sem):
    pairs = ((gg_in, gg_out), (gu_in, gu_out), (gd_in, gd_out), (gi_in, gi_out))
    copies = [pltpu.make_async_copy(src, dst, sem.at[i]) for i, (src, dst) in enumerate(pairs)]
    for copy in copies:
        copy.start()
    for copy in copies:
        copy.wait()


def body(tokens, cotangent, gate_weight, up_weight, down_weight):
    vmem = pl.BlockSpec(memory_space=pltpu.VMEM)
    hbm = pl.BlockSpec(memory_space=pl.ANY)
    dma = pltpu.SemaphoreType.DMA
    shapes = ((1024, 512), (1024, 512), (512, 1024), (32, 1024))
    results = pl.pallas_call(
        kernel,
        out_shape=tuple(pltpu.VMEM(shape, BF16) for shape in shapes),
        in_specs=[hbm] * 5,
        out_specs=(vmem,) * 4,
        scratch_shapes=[
            pltpu.VMEM((2, 16, 64, 1024), BF16),
            pltpu.VMEM((1024, 1024), BF16),
            pltpu.VMEM((512, 1024), BF16),
            pltpu.VMEM((8, 128, WIDE), F32),
            pltpu.VMEM((8, 2, 4, 16, WIDE), BF16),
            pltpu.VMEM((8, 2, 4, 16, WIDE), BF16),
            pltpu.VMEM((8, 128, 1024), BF16),
            pltpu.VMEM((8, 128, 512), BF16),
            pltpu.VMEM((1024, 1024), F32),
            pltpu.VMEM((512, 1024), F32),
            pltpu.VMEM((8, 2, 32, 1024), F32),
            pltpu.VMEM((8, 2, 32, 1024), F32),
            pltpu.VMEM((16, 32, 1024), BF16),
            pltpu.VMEM((16, 32, 1024), BF16),
            pltpu.VMEM((8, 2, 32, 1024), F32),
            dma((5,)),
            dma((18,)), dma((18,)),
            dma((16,)), dma((16,)),
            dma((8, 2, 4)), dma((8, 2, 4)),
            dma((8, 2, 4)), dma((8, 2, 4)),
            dma((2, 2, 4)), dma((2, 2, 4)),
            dma((8,)), dma((8,)),
            dma((16,)), dma((16,)),
        ],
        compiler_params=pltpu.CompilerParams(
            collective_id=0, has_side_effects=True, vmem_limit_bytes=56 * 2**20
        ),
    )(tokens, cotangent, gate_weight, up_weight, down_weight)
    return pl.pallas_call(
        flush,
        out_shape=tuple(jax.ShapeDtypeStruct(shape, BF16) for shape in shapes),
        in_specs=[vmem] * 4,
        out_specs=(hbm,) * 4,
        scratch_shapes=[dma((4,))],
        compiler_params=pltpu.CompilerParams(vmem_limit_bytes=8 * 2**20),
    )(*results)


def solution(mesh):
    placed = (P("row", "col"), P("row", "col"), P("col", "row"), P("col", "row"), P("row", "col"))
    return jax.shard_map(
        body,
        mesh=mesh,
        in_specs=placed,
        out_specs=(P("col", "row"), P("col", "row"), P("row", "col"), P("row", "col")),
        check_vma=False,
    )
```

```python
import jax
import jax.numpy as jnp
from jax import lax
from jax.experimental import pallas as pl
from jax.experimental.pallas import tpu as pltpu
from jax.sharding import PartitionSpec as P

MESH = pl.DeviceIdType.MESH
F32, BF16 = jnp.float32, jnp.bfloat16
INNER = (((1,), (1,)), ((), ()))
OUTER = (((0,), (0,)), ((), ()))
SCALE = 2.0**51
WIDE, HALF = 1536, 768
OWN = (0, 0)
SLOTS = (
    (0, 3), (1, 1), (1, 3), (3, 1), (3, 3), (2, 0), (0, 2), (2, 1),
    (2, 3), (1, 2), (3, 2), (2, 2), (0, 0), (1, 0), (0, 1), (3, 0),
)
PLACE = {offset: slot for slot, offset in enumerate(SLOTS)}
FIRST = tuple((OWN, to, 0, 32) for to in ((3, 0), (1, 0), (0, 3), (0, 1)))
SECOND = (
    ((0, 1), (3, 0), 0, 32), ((0, 3), (1, 0), 0, 32), ((1, 0), (0, 1), 0, 32), ((3, 0), (0, 3), 0, 32),
    ((1, 0), (3, 0), 0, 16), ((3, 0), (1, 0), 16, 16), ((0, 1), (0, 3), 0, 16), ((0, 3), (0, 1), 16, 16),
)
THIRD = (
    ((1, 1), (3, 0), 0, 32), ((3, 3), (1, 0), 0, 32), ((1, 1), (0, 3), 0, 32), ((3, 3), (0, 1), 0, 32),
    (OWN, (2, 2), 0, 32),
)
ROUNDS = (FIRST, SECOND, THIRD)
ARRIVALS = (
    ((1, 0), (3, 0), (0, 1), (0, 3)),
    ((1, 1), (1, 3), (3, 1), (3, 3)),
    ((2, 0), (0, 2)),
    ((2, 1), (2, 3), (1, 2), (3, 2)),
    ((2, 2),),
)
ROWS, PART, RED0, RED1, RED2, RED3, RED4, GAT1, GAT2, GAT3, GAT4, GIVE, SEND = range(13)
HID0, HID1, HID2, HID3, HID4, PAST, DOWN, LAST = range(13, 21)
ORDER = (
    (ROWS, 0), (PART, 6), (RED0, 6), (PART, 7), (RED0, 7), (ROWS, 1), (RED1, 6), (RED1, 7),
    (ROWS, 2), (PART, 0), (RED0, 0), (PART, 1), (RED0, 1), (PART, 2), (RED0, 2), (RED2, 6),
    (RED2, 7), (RED1, 0), (ROWS, 3), (RED1, 1), (PART, 3), (ROWS, 4), (RED0, 3), (RED1, 2),
    (RED3, 6), (PART, 4), (RED0, 4), (RED3, 7), (PART, 5), (RED0, 5), (RED2, 0), (RED2, 1),
    (RED1, 3), (RED2, 2), (RED1, 4), (RED1, 5), (RED3, 0), (RED3, 1), (RED2, 3), (RED3, 2),
    (RED2, 4), (RED2, 5), (RED4, 0), (RED4, 1), (RED3, 3), (RED4, 2), (RED3, 4), (RED3, 5),
    (GAT1, 0), (GAT1, 1), (RED4, 3), (GAT1, 2), (RED4, 4), (RED4, 5), (GAT2, 0), (GAT2, 1),
    (GAT1, 3), (GAT2, 2), (GAT1, 4), (GAT1, 5), (GAT3, 0), (GAT3, 1), (GAT2, 3), (RED4, 6),
    (RED4, 7), (GAT2, 4), (GAT3, 2), (GAT2, 5), (GAT4, 0), (GIVE, 0), (GAT4, 1), (GAT3, 3),
    (GIVE, 1), (GAT1, 6), (GAT1, 7), (SEND, 0), (HID0, 0), (GAT3, 4), (HID0, 1), (GAT4, 2),
    (GIVE, 2), (GAT3, 5), (GAT4, 3), (SEND, 1), (GIVE, 3), (GAT2, 6), (GAT2, 7), (PAST, 0),
    (SEND, 2), (PAST, 1), (GAT4, 4), (SEND, 3), (HID1, 0), (GIVE, 4), (HID1, 1), (GAT4, 5),
    (GIVE, 5), (GAT3, 6), (PAST, 2), (GAT3, 7), (SEND, 4), (PAST, 3), (SEND, 5), (HID2, 0),
    (HID2, 1), (GAT4, 6), (GIVE, 6), (GAT4, 7), (GIVE, 7), (PAST, 4), (SEND, 6), (HID3, 0),
    (PAST, 5), (SEND, 7), (HID3, 1), (PAST, 6), (PAST, 7), (HID4, 0), (DOWN, 0), (DOWN, 1),
    (HID4, 1), (DOWN, 2), (DOWN, 3), (LAST, 0),
)


def encode(value):
    scaled = value * SCALE
    return (scaled * jnp.abs(scaled)).astype(BF16)


def decode(coded):
    wide = coded.astype(F32)
    return wide * lax.rsqrt(jnp.maximum(jnp.abs(wide), 1e-37)) * (1.0 / SCALE)


def product(a, b, dims=(((1,), (0,)), ((), ()))):
    return lax.dot_general(a, b, dims, preferred_element_type=F32)


def kernel(
    tok_ref, cot_ref, wg_ref, wu_ref, wd_ref,
    gg_ref, gu_ref, gd_ref, gi_ref,
    rows, both, down, part, sent, got, hid, hidden, acc, accd, give, take, out16, in16, local,
    load_s, rows_s, rows_r, pair_s, pair_r, red_s, red_r, gat_s, gat_r, hid_s, hid_r, give_s, give_r, gi_s, gi_r,
):
    row, z = lax.axis_index("row"), lax.axis_index("col")
    x, y, c = row // 8, (row // 2) % 4, row % 2

    def plane(offset):
        return (((x + offset[0]) % 4) * 4 + (y + offset[1]) % 4) * 2 + c, z

    partner = (row + 1 - 2 * c, z)
    side = ((row, (z + 1) % 8), (row, (z + 7) % 8))

    def remote(src, dst, s, r, device):
        return pltpu.make_async_remote_copy(
            src_ref=src, dst_ref=dst, send_sem=s, recv_sem=r, device_id=device, device_id_type=MESH
        )

    barrier = pltpu.get_barrier_semaphore()
    peers = [side[0], side[1], partner] + [plane(offset) for offset in SLOTS if offset != OWN]
    for peer in peers:
        pl.semaphore_signal(barrier, inc=1, device_id=peer, device_id_type=MESH)
    own = PLACE[OWN]
    loads = [
        pltpu.make_async_copy(tok_ref, rows.at[0, own, 0:32], load_s.at[0]),
        pltpu.make_async_copy(cot_ref, rows.at[1, own, 0:32], load_s.at[1]),
        pltpu.make_async_copy(wg_ref, both.at[:, 0:512], load_s.at[2]),
        pltpu.make_async_copy(wu_ref, both.at[:, 512:1024], load_s.at[3]),
        pltpu.make_async_copy(wd_ref, down, load_s.at[4]),
    ]
    for load in loads:
        load.start()
    for load in loads[:2]:
        load.wait()
    pl.semaphore_wait(barrier, len(peers))

    def rows_copy(source, to, first, count):
        lands = PLACE[((source[0] - to[0]) % 4, (source[1] - to[1]) % 4)]
        sem = lands if first == 0 else 16 + (PLACE[(0, 2)] == lands)
        return remote(
            rows.at[:, PLACE[source], first : first + count],
            rows.at[:, lands, first : first + count],
            rows_s.at[sem],
            rows_r.at[sem],
            plane(to),
        )

    def pair_copy(slot, src, dst):
        return remote(
            rows.at[:, slot, src : src + 32], rows.at[:, slot, dst : dst + 32], pair_s.at[slot], pair_r.at[slot], partner
        )

    def rows_send(k):
        for send in ROUNDS[k]:
            rows_copy(*send).start()

    def rows_step(k):
        for send in (send for sends in ROUNDS for send in sends):
            source, to, first, count = send
            offset = ((source[0] - to[0]) % 4, (source[1] - to[1]) % 4)
            if offset in ARRIVALS[k]:
                ref = rows.at[:, PLACE[offset], first : first + count]
                sem = PLACE[offset] if first == 0 else 16 + (offset == (0, 2))
                remote(ref, ref, rows_s.at[sem], rows_r.at[sem], partner).wait_recv()
        if k < 2:
            rows_send(k + 1)
        for offset in ARRIVALS[k]:
            pair_copy(PLACE[offset], 0, 32).start()

    def partials(u):
        for slot in (2 * u, 2 * u + 1):
            pair_copy(slot, 32, 32).wait_recv()
        tok = rows[0, 2 * u : 2 * u + 2].reshape(128, 1024)
        cot = rows[1, 2 * u : 2 * u + 2].reshape(128, 1024)
        part[u, :, 0:1024] = product(tok, both[...])
        part[u, :, 1024:1536] = product(cot, down[...], INNER)

    def block(o):
        return pl.ds(pl.multiple_of((o % 8) * 16, 16), 16)

    def lanes(way):
        return pl.ds(way * HALF, HALF)

    def red_copy(u, way, h):
        if h == 0:
            src, dst = sent.at[u, way, h, :, lanes(way)], got.at[u, way, h, :, lanes(way)]
        else:
            src, dst = sent.at[u, way, h], got.at[u, way, h]
        return remote(src, dst, red_s.at[u, way, h], red_r.at[u, way, h], side[way])

    def red_first(u):
        for way in range(2):
            sent[u, way, 0, :, lanes(way)] = encode(part[u, block(z + 4), lanes(way)])
            red_copy(u, way, 0).start()

    def red_hop(u, h):
        for way in range(2):
            o = z + 4 - h if way == 0 else z + 4 + h
            if h == 1:
                sent[u, way, h, :, lanes(1 - way)] = encode(part[u, block(o), lanes(1 - way)])
                red_copy(u, way, 0).wait_recv()
                value = part[u, block(o), lanes(way)] + decode(got[u, way, 0, :, lanes(way)])
                sent[u, way, h, :, lanes(way)] = encode(value)
            else:
                red_copy(u, way, h - 1).wait_recv()
                sent[u, way, h] = encode(part[u, block(o), :] + decode(got[u, way, h - 1]))
            red_copy(u, way, h).start()
        for way in range(2):
            red_copy(u, way, h - 1).wait_send()

    def red_last(u):
        for way in range(2):
            red_copy(u, way, 3).wait_recv()
        gate, up, back = [
            part[u, block(z), span] + decode(got[u, 0, 3, :, span]) + decode(got[u, 1, 3, :, span])
            for span in (pl.ds(0, 512), pl.ds(512, 512), pl.ds(1024, 512))
        ]
        sig = 1.0 / (1.0 + jnp.exp(-gate))
        hid[u, block(z), 0:512] = (back * up * sig * (1.0 + gate * (1.0 - sig))).astype(BF16)
        hid[u, block(z), 512:1024] = (back * gate * sig).astype(BF16)
        hidden[u, block(z), :] = (gate * sig * up).astype(BF16)
        for way in range(2):
            gat_copy(u, way, 0, z).start()
        for way in range(2):
            red_copy(u, way, 3).wait_send()

    def gat_copy(u, way, a, o):
        ref = hid.at[u, block(o), pl.ds(way * 512, 512)] if a == 3 else hid.at[u, block(o)]
        return remote(ref, ref, gat_s.at[u, way, a], gat_r.at[u, way, a], side[way])

    def origin(way, a):
        return z + 8 - a if way == 0 else z + a

    def gat_hop(u, a):
        for way in range(2):
            gat_copy(u, way, a - 1, origin(way, a)).wait_recv()
            gat_copy(u, way, a, origin(way, a)).start()
        for way in range(2):
            gat_copy(u, way, a - 1, origin(way, a - 1)).wait_send()

    def gat_last(u):
        for way in range(2):
            gat_copy(u, way, 3, origin(way, 4)).wait_recv()
        for way in range(2):
            gat_copy(u, way, 3, origin(way, 3)).wait_send()

    def hid_copy(g, way, a, o):
        span = pl.ds(way * 256, 256) if a == 3 else pl.ds(0, 512)
        ref = hidden.at[4 * g : 4 * g + 4, block(o), span]
        return remote(ref, ref, hid_s.at[g, way, a], hid_r.at[g, way, a], side[way])

    def hid_hop(g, a):
        for way in range(2):
            if a > 0:
                hid_copy(g, way, a - 1, origin(way, a)).wait_recv()
            if a < 4:
                hid_copy(g, way, a, origin(way, a)).start()
        if a > 0:
            for way in range(2):
                hid_copy(g, way, a - 1, origin(way, a - 1)).wait_send()

    def give_copy(u):
        return remote(give.at[u], take.at[u], give_s.at[u], give_r.at[u], partner)

    def input_first(u):
        value = product(hid[u], both[...], INNER).reshape(2, 64, 1024)
        give[u] = value[:, 32:64]
        give_copy(u).start()
        local[u] = value[:, 0:32]

    def gi_copy(slot):
        return remote(out16.at[slot], in16.at[slot], gi_s.at[slot], gi_r.at[slot], plane(SLOTS[slot]))

    def input_second(u):
        give_copy(u).wait_recv()
        for i in range(2):
            slot = 2 * u + i
            value = (local[u, i] + take[u, i]).astype(BF16)
            if slot == own:
                in16[slot] = value
            else:
                out16[slot] = value
                gi_copy(slot).start()

    def input_last():
        total = in16[own].astype(F32)
        for slot in range(16):
            if slot != own:
                gi_copy(slot).wait_recv()
                total = total + in16[slot].astype(F32)
        gi_ref[...] = total.astype(BF16)

    def weights(i, half):
        span = pl.ds(i * 256, 256)
        left = rows[0, 8 * half : 8 * half + 8, :, span].reshape(512, 256)
        value = product(left, hid[4 * half : 4 * half + 4].reshape(512, 1024), OUTER)
        if half == 0:
            acc[span, :] = value
        else:
            value = acc[span, :] + value
            gg_ref[span, :] = value[:, 0:512].astype(BF16)
            gu_ref[span, :] = value[:, 512:1024].astype(BF16)

    def weights_down(i, half):
        span = pl.ds(i * 256, 256)
        left = hidden[4 * half : 4 * half + 4, :, span].reshape(512, 256)
        value = product(left, rows[1, 8 * half : 8 * half + 8].reshape(512, 1024), OUTER)
        if half == 0:
            accd[span, :] = value
        else:
            gd_ref[span, :] = (accd[span, :] + value).astype(BF16)

    pair_copy(own, 0, 32).start()
    rows_send(0)
    for load in loads[2:]:
        load.wait()
    for step, n in ORDER:
        if step == ROWS:
            rows_step(n)
        elif step == PART:
            partials(n)
        elif step == RED0:
            red_first(n)
        elif step < RED4:
            red_hop(n, step - RED0)
        elif step == RED4:
            red_last(n)
        elif step < GAT4:
            gat_hop(n, step - GAT1 + 1)
        elif step == GAT4:
            gat_last(n)
        elif step == GIVE:
            input_first(n)
        elif step == SEND:
            input_second(n)
        elif step == LAST:
            input_last()
        elif step < PAST:
            hid_hop(n, step - HID0)
        elif step == PAST:
            weights(n % 4, n // 4)
        else:
            weights_down(n % 2, n // 2)

    for u in range(8):
        give_copy(u).wait_send()
    for slot in range(16):
        pair_copy(slot, 0, 32).wait_send()
        if slot != own:
            gi_copy(slot).wait_send()
    for sends in ROUNDS:
        for send in sends:
            rows_copy(*send).wait_send()


def flush(gg_in, gu_in, gd_in, gi_in, gg_out, gu_out, gd_out, gi_out, sem):
    pairs = ((gg_in, gg_out), (gu_in, gu_out), (gd_in, gd_out), (gi_in, gi_out))
    copies = [pltpu.make_async_copy(src, dst, sem.at[i]) for i, (src, dst) in enumerate(pairs)]
    for copy in copies:
        copy.start()
    for copy in copies:
        copy.wait()


def body(tokens, cotangent, gate_weight, up_weight, down_weight):
    vmem = pl.BlockSpec(memory_space=pltpu.VMEM)
    hbm = pl.BlockSpec(memory_space=pl.ANY)
    dma = pltpu.SemaphoreType.DMA
    shapes = ((1024, 512), (1024, 512), (512, 1024), (32, 1024))
    results = pl.pallas_call(
        kernel,
        out_shape=tuple(pltpu.VMEM(shape, BF16) for shape in shapes),
        in_specs=[hbm] * 5,
        out_specs=(vmem,) * 4,
        scratch_shapes=[
            pltpu.VMEM((2, 16, 64, 1024), BF16),
            pltpu.VMEM((1024, 1024), BF16),
            pltpu.VMEM((512, 1024), BF16),
            pltpu.VMEM((8, 128, WIDE), F32),
            pltpu.VMEM((8, 2, 4, 16, WIDE), BF16),
            pltpu.VMEM((8, 2, 4, 16, WIDE), BF16),
            pltpu.VMEM((8, 128, 1024), BF16),
            pltpu.VMEM((8, 128, 512), BF16),
            pltpu.VMEM((1024, 1024), F32),
            pltpu.VMEM((512, 1024), F32),
            pltpu.VMEM((8, 2, 32, 1024), F32),
            pltpu.VMEM((8, 2, 32, 1024), F32),
            pltpu.VMEM((16, 32, 1024), BF16),
            pltpu.VMEM((16, 32, 1024), BF16),
            pltpu.VMEM((8, 2, 32, 1024), F32),
            dma((5,)),
            dma((18,)), dma((18,)),
            dma((16,)), dma((16,)),
            dma((8, 2, 4)), dma((8, 2, 4)),
            dma((8, 2, 4)), dma((8, 2, 4)),
            dma((2, 2, 4)), dma((2, 2, 4)),
            dma((8,)), dma((8,)),
            dma((16,)), dma((16,)),
        ],
        compiler_params=pltpu.CompilerParams(
            collective_id=0, has_side_effects=True, vmem_limit_bytes=56 * 2**20
        ),
    )(tokens, cotangent, gate_weight, up_weight, down_weight)
    return pl.pallas_call(
        flush,
        out_shape=tuple(jax.ShapeDtypeStruct(shape, BF16) for shape in shapes),
        in_specs=[vmem] * 4,
        out_specs=(hbm,) * 4,
        scratch_shapes=[dma((4,))],
        compiler_params=pltpu.CompilerParams(vmem_limit_bytes=8 * 2**20),
    )(*results)


def solution(mesh):
    placed = (P("row", "col"), P("row", "col"), P("col", "row"), P("col", "row"), P("row", "col"))
    return jax.shard_map(
        body,
        mesh=mesh,
        in_specs=placed,
        out_specs=(P("col", "row"), P("col", "row"), P("row", "col"), P("row", "col")),
        check_vma=False,
    )
```

```python
import jax
import jax.numpy as jnp
from jax import lax
from jax.experimental import pallas as pl
from jax.experimental.pallas import tpu as pltpu
from jax.sharding import PartitionSpec as P

MESH = pl.DeviceIdType.MESH
F32, BF16 = jnp.float32, jnp.bfloat16
INNER = (((1,), (1,)), ((), ()))
OUTER = (((0,), (0,)), ((), ()))
SCALE = 2.0**51
WIDE, HALF = 1536, 768
OWN = (0, 0)
SLOTS = (
    (0, 3), (1, 1), (1, 3), (3, 1), (3, 3), (2, 0), (0, 2), (2, 1),
    (2, 3), (1, 2), (3, 2), (2, 2), (0, 0), (1, 0), (0, 1), (3, 0),
)
PLACE = {offset: slot for slot, offset in enumerate(SLOTS)}
FIRST = tuple((OWN, to, 0, 32) for to in ((3, 0), (1, 0), (0, 3), (0, 1)))
SECOND = (
    ((0, 1), (3, 0), 0, 32), ((0, 3), (1, 0), 0, 32), ((1, 0), (0, 1), 0, 32), ((3, 0), (0, 3), 0, 32),
    ((1, 0), (3, 0), 0, 16), ((3, 0), (1, 0), 16, 16), ((0, 1), (0, 3), 0, 16), ((0, 3), (0, 1), 16, 16),
)
THIRD = (
    ((1, 1), (3, 0), 0, 32), ((3, 3), (1, 0), 0, 32), ((1, 1), (0, 3), 0, 32), ((3, 3), (0, 1), 0, 32),
    (OWN, (2, 2), 0, 32),
)
ROUNDS = (FIRST, SECOND, THIRD)
ARRIVALS = (
    ((1, 0), (0, 1), (3, 0), (0, 3)),
    ((1, 1), (1, 3), (3, 1), (3, 3)),
    ((2, 0), (0, 2)),
    ((2, 1), (2, 3), (1, 2), (3, 2)),
    ((2, 2),),
)
ROWS, PART, RED0, RED1, RED2, RED3, RED4, GAT1, GAT2, GAT3, GAT4, GIVE, SEND = range(13)
HID0, HID1, HID2, HID3, HID4, PAST, DOWN, LAST, DRAIN = range(13, 22)
ORDER = (
    (ROWS, 0), (PART, 6), (RED0, 6), (PART, 7), (RED0, 7), (ROWS, 1), (RED1, 6), (RED1, 7),
    (ROWS, 2), (PART, 0), (RED0, 0), (PART, 1), (RED0, 1), (PART, 2), (RED0, 2), (RED2, 6),
    (RED2, 7), (RED1, 0), (ROWS, 3), (RED1, 1), (PART, 3), (ROWS, 4), (RED0, 3), (RED1, 2),
    (RED3, 6), (PART, 4), (RED0, 4), (RED3, 7), (PART, 5), (RED0, 5), (RED2, 0), (RED2, 1),
    (RED1, 3), (RED2, 2), (RED1, 4), (RED1, 5), (RED3, 0), (RED3, 1), (RED2, 3), (RED3, 2),
    (RED2, 4), (RED2, 5), (RED4, 0), (RED4, 1), (RED3, 3), (RED4, 2), (RED3, 4), (RED3, 5),
    (GAT1, 0), (GAT1, 1), (RED4, 3), (GAT1, 2), (RED4, 4), (RED4, 5), (GAT2, 0), (GAT2, 1),
    (GAT1, 3), (GAT2, 2), (GAT1, 4), (GAT1, 5), (GAT3, 0), (GAT3, 1), (GAT2, 3), (RED4, 6),
    (RED4, 7), (GAT2, 4), (GAT3, 2), (GAT2, 5), (GAT4, 0), (GIVE, 0), (GAT4, 1), (GAT3, 3),
    (GIVE, 1), (GAT1, 6), (GAT1, 7), (SEND, 0), (HID0, 0), (GAT3, 4), (HID0, 1), (DRAIN, 0), (GAT4, 2),
    (GIVE, 2), (GAT3, 5), (GAT4, 3), (SEND, 1), (GIVE, 3), (GAT2, 6), (GAT2, 7), (PAST, 0),
    (SEND, 2), (PAST, 1), (GAT4, 4), (SEND, 3), (HID1, 0), (GIVE, 4), (HID1, 1), (DRAIN, 1), (GAT4, 5),
    (GIVE, 5), (GAT3, 6), (PAST, 2), (GAT3, 7), (SEND, 4), (PAST, 3), (SEND, 5), (HID2, 0),
    (HID2, 1), (GAT4, 6), (GIVE, 6), (GAT4, 7), (GIVE, 7), (PAST, 4), (SEND, 6), (HID3, 0),
    (PAST, 5), (SEND, 7), (HID3, 1), (PAST, 6), (PAST, 7), (HID4, 0), (DOWN, 0), (DOWN, 1),
    (LAST, 1), (HID4, 1), (DOWN, 2), (DOWN, 3), (LAST, 0),
)


def encode(value):
    scaled = value * SCALE
    return (scaled * jnp.abs(scaled)).astype(BF16)


def decode(coded):
    wide = coded.astype(F32)
    return wide * lax.rsqrt(jnp.maximum(jnp.abs(wide), 1e-37)) * (1.0 / SCALE)


def product(a, b, dims=(((1,), (0,)), ((), ()))):
    return lax.dot_general(a, b, dims, preferred_element_type=F32)


def kernel(
    tok_ref, cot_ref, wg_ref, wu_ref, wd_ref,
    gg_ref, gu_ref, gd_ref, gi_ref,
    rows, both, down, part, sent, got, hid, hidden, acc, accd, give, take, out16, in16, local,
    load_s, rows_s, rows_r, pair_s, pair_r, red_s, red_r, gat_s, gat_r, hid_s, hid_r, give_s, give_r, gi_s, gi_r,
):
    row, z = lax.axis_index("row"), lax.axis_index("col")
    x, y, c = row // 8, (row // 2) % 4, row % 2

    def plane(offset):
        return (((x + offset[0]) % 4) * 4 + (y + offset[1]) % 4) * 2 + c, z

    partner = (row + 1 - 2 * c, z)
    side = ((row, (z + 1) % 8), (row, (z + 7) % 8))

    def remote(src, dst, s, r, device):
        return pltpu.make_async_remote_copy(
            src_ref=src, dst_ref=dst, send_sem=s, recv_sem=r, device_id=device, device_id_type=MESH
        )

    barrier = pltpu.get_barrier_semaphore()
    peers = [side[0], side[1], partner] + [plane(offset) for offset in SLOTS if offset != OWN]
    for peer in peers:
        pl.semaphore_signal(barrier, inc=1, device_id=peer, device_id_type=MESH)
    own = PLACE[OWN]
    loads = [
        pltpu.make_async_copy(tok_ref, rows.at[0, own, 0:32], load_s.at[0]),
        pltpu.make_async_copy(cot_ref, rows.at[1, own, 0:32], load_s.at[1]),
        pltpu.make_async_copy(wg_ref, both.at[:, 0:512], load_s.at[2]),
        pltpu.make_async_copy(wu_ref, both.at[:, 512:1024], load_s.at[3]),
        pltpu.make_async_copy(wd_ref, down, load_s.at[4]),
    ]
    for load in loads:
        load.start()
    for load in loads[:2]:
        load.wait()
    pl.semaphore_wait(barrier, len(peers))

    def rows_copy(source, to, first, count):
        lands = PLACE[((source[0] - to[0]) % 4, (source[1] - to[1]) % 4)]
        sem = lands if first == 0 else 16 + (PLACE[(0, 2)] == lands)
        return remote(
            rows.at[:, PLACE[source], first : first + count],
            rows.at[:, lands, first : first + count],
            rows_s.at[sem],
            rows_r.at[sem],
            plane(to),
        )

    def pair_copy(slot, src, dst):
        return remote(
            rows.at[:, slot, src : src + 32], rows.at[:, slot, dst : dst + 32], pair_s.at[slot], pair_r.at[slot], partner
        )

    def rows_send(k):
        for send in ROUNDS[k]:
            rows_copy(*send).start()

    def rows_step(k):
        for offset in ARRIVALS[k]:
            for source, to, first, count in (send for sends in ROUNDS for send in sends):
                if offset == ((source[0] - to[0]) % 4, (source[1] - to[1]) % 4):
                    ref = rows.at[:, PLACE[offset], first : first + count]
                    sem = PLACE[offset] if first == 0 else 16 + (offset == (0, 2))
                    remote(ref, ref, rows_s.at[sem], rows_r.at[sem], partner).wait_recv()
            pair_copy(PLACE[offset], 0, 32).start()
        if k < 2:
            rows_send(k + 1)

    def partials(u):
        for slot in (2 * u, 2 * u + 1):
            pair_copy(slot, 32, 32).wait_recv()
        tok = rows[0, 2 * u : 2 * u + 2].reshape(128, 1024)
        cot = rows[1, 2 * u : 2 * u + 2].reshape(128, 1024)
        part[u, :, 0:1024] = product(tok, both[...])
        part[u, :, 1024:1536] = product(cot, down[...], INNER)

    def block(o):
        return pl.ds(pl.multiple_of((o % 8) * 16, 16), 16)

    def lanes(way):
        return pl.ds(way * HALF, HALF)

    def red_copy(u, way, h):
        if h == 0:
            src, dst = sent.at[u, way, h, :, lanes(way)], got.at[u, way, h, :, lanes(way)]
        else:
            src, dst = sent.at[u, way, h], got.at[u, way, h]
        return remote(src, dst, red_s.at[u, way, h], red_r.at[u, way, h], side[way])

    def red_first(u):
        for way in range(2):
            sent[u, way, 0, :, lanes(way)] = encode(part[u, block(z + 4), lanes(way)])
            red_copy(u, way, 0).start()

    def red_hop(u, h):
        for way in range(2):
            o = z + 4 - h if way == 0 else z + 4 + h
            if h == 1:
                sent[u, way, h, :, lanes(1 - way)] = encode(part[u, block(o), lanes(1 - way)])
                red_copy(u, way, 0).wait_recv()
                value = part[u, block(o), lanes(way)] + decode(got[u, way, 0, :, lanes(way)])
                sent[u, way, h, :, lanes(way)] = encode(value)
            else:
                red_copy(u, way, h - 1).wait_recv()
                sent[u, way, h] = encode(part[u, block(o), :] + decode(got[u, way, h - 1]))
            red_copy(u, way, h).start()
        for way in range(2):
            red_copy(u, way, h - 1).wait_send()

    def red_last(u):
        for way in range(2):
            red_copy(u, way, 3).wait_recv()
        gate, up, back = [
            part[u, block(z), span] + decode(got[u, 0, 3, :, span]) + decode(got[u, 1, 3, :, span])
            for span in (pl.ds(0, 512), pl.ds(512, 512), pl.ds(1024, 512))
        ]
        sig = 1.0 / (1.0 + jnp.exp(-gate))
        hid[u, block(z), 0:512] = (back * up * sig * (1.0 + gate * (1.0 - sig))).astype(BF16)
        hid[u, block(z), 512:1024] = (back * gate * sig).astype(BF16)
        hidden[u, block(z), :] = (gate * sig * up).astype(BF16)
        for way in range(2):
            gat_copy(u, way, 0, z).start()
        for way in range(2):
            red_copy(u, way, 3).wait_send()

    def gat_copy(u, way, a, o):
        ref = hid.at[u, block(o), pl.ds(way * 512, 512)] if a == 3 else hid.at[u, block(o)]
        return remote(ref, ref, gat_s.at[u, way, a], gat_r.at[u, way, a], side[way])

    def origin(way, a):
        return z + 8 - a if way == 0 else z + a

    def gat_hop(u, a):
        for way in range(2):
            gat_copy(u, way, a - 1, origin(way, a)).wait_recv()
            gat_copy(u, way, a, origin(way, a)).start()
        for way in range(2):
            gat_copy(u, way, a - 1, origin(way, a - 1)).wait_send()

    def gat_last(u):
        for way in range(2):
            gat_copy(u, way, 3, origin(way, 4)).wait_recv()
        for way in range(2):
            gat_copy(u, way, 3, origin(way, 3)).wait_send()

    def hid_copy(g, way, a, o):
        span = pl.ds(way * 256, 256) if a == 3 else pl.ds(0, 512)
        ref = hidden.at[4 * g : 4 * g + 4, block(o), span]
        return remote(ref, ref, hid_s.at[g, way, a], hid_r.at[g, way, a], side[way])

    def hid_hop(g, a):
        for way in range(2):
            if a > 0:
                hid_copy(g, way, a - 1, origin(way, a)).wait_recv()
            if a < 4:
                hid_copy(g, way, a, origin(way, a)).start()
        if a > 0:
            for way in range(2):
                hid_copy(g, way, a - 1, origin(way, a - 1)).wait_send()

    def give_copy(u):
        return remote(give.at[u], take.at[u], give_s.at[u], give_r.at[u], partner)

    def input_first(u):
        value = product(hid[u], both[...], INNER).reshape(2, 64, 1024)
        give[u] = value[:, 32:64]
        give_copy(u).start()
        local[u] = value[:, 0:32]

    def gi_copy(slot):
        return remote(out16.at[slot], in16.at[slot], gi_s.at[slot], gi_r.at[slot], plane(SLOTS[slot]))

    def input_second(u):
        give_copy(u).wait_recv()
        give_copy(u).wait_send()
        for i in range(2):
            slot = 2 * u + i
            value = (local[u, i] + take[u, i]).astype(BF16)
            if slot == own:
                in16[slot] = value
            else:
                out16[slot] = value
                gi_copy(slot).start()

    def input_last(early):
        slots = range(0, 12) if early else range(12, 16)
        total = jnp.zeros((32, 1024), F32) if early else local[0, 0]
        for slot in slots:
            if slot != own:
                gi_copy(slot).wait_recv()
            total = total + in16[slot].astype(F32)
        if early:
            local[0, 0] = total
        else:
            gi_ref[...] = total.astype(BF16)
        for slot in slots:
            if slot != own:
                gi_copy(slot).wait_send()

    def weights(i, half):
        span = pl.ds(i * 256, 256)
        left = rows[0, 8 * half : 8 * half + 8, :, span].reshape(512, 256)
        value = product(left, hid[4 * half : 4 * half + 4].reshape(512, 1024), OUTER)
        if half == 0:
            acc[span, :] = value
        else:
            value = acc[span, :] + value
            gg_ref[span, :] = value[:, 0:512].astype(BF16)
            gu_ref[span, :] = value[:, 512:1024].astype(BF16)

    def weights_down(i, half):
        span = pl.ds(i * 256, 256)
        left = hidden[4 * half : 4 * half + 4, :, span].reshape(512, 256)
        value = product(left, rows[1, 8 * half : 8 * half + 8].reshape(512, 1024), OUTER)
        if half == 0:
            accd[span, :] = value
        else:
            gd_ref[span, :] = (accd[span, :] + value).astype(BF16)

    pair_copy(own, 0, 32).start()
    rows_send(0)
    for load in loads[2:]:
        load.wait()
    for step, n in ORDER:
        if step == ROWS:
            rows_step(n)
        elif step == PART:
            partials(n)
        elif step == RED0:
            red_first(n)
        elif step < RED4:
            red_hop(n, step - RED0)
        elif step == RED4:
            red_last(n)
        elif step < GAT4:
            gat_hop(n, step - GAT1 + 1)
        elif step == GAT4:
            gat_last(n)
        elif step == GIVE:
            input_first(n)
        elif step == SEND:
            input_second(n)
        elif step == LAST:
            input_last(n == 1)
        elif step == DRAIN and n == 0:
            for sends in ROUNDS:
                for send in sends:
                    rows_copy(*send).wait_send()
        elif step == DRAIN:
            for slot in range(16):
                pair_copy(slot, 0, 32).wait_send()
        elif step < PAST:
            hid_hop(n, step - HID0)
        elif step == PAST:
            weights(n % 4, n // 4)
        else:
            weights_down(n % 2, n // 2)


def flush(gg_in, gu_in, gd_in, gi_in, gg_out, gu_out, gd_out, gi_out, sem):
    pairs = ((gg_in, gg_out), (gu_in, gu_out), (gd_in, gd_out), (gi_in, gi_out))
    copies = [pltpu.make_async_copy(src, dst, sem.at[i]) for i, (src, dst) in enumerate(pairs)]
    for copy in copies:
        copy.start()
    for copy in copies:
        copy.wait()


def body(tokens, cotangent, gate_weight, up_weight, down_weight):
    vmem = pl.BlockSpec(memory_space=pltpu.VMEM)
    hbm = pl.BlockSpec(memory_space=pl.ANY)
    dma = pltpu.SemaphoreType.DMA
    shapes = ((1024, 512), (1024, 512), (512, 1024), (32, 1024))
    results = pl.pallas_call(
        kernel,
        out_shape=tuple(pltpu.VMEM(shape, BF16) for shape in shapes),
        in_specs=[hbm] * 5,
        out_specs=(vmem,) * 4,
        scratch_shapes=[
            pltpu.VMEM((2, 16, 64, 1024), BF16),
            pltpu.VMEM((1024, 1024), BF16),
            pltpu.VMEM((512, 1024), BF16),
            pltpu.VMEM((8, 128, WIDE), F32),
            pltpu.VMEM((8, 2, 4, 16, WIDE), BF16),
            pltpu.VMEM((8, 2, 4, 16, WIDE), BF16),
            pltpu.VMEM((8, 128, 1024), BF16),
            pltpu.VMEM((8, 128, 512), BF16),
            pltpu.VMEM((1024, 1024), F32),
            pltpu.VMEM((512, 1024), F32),
            pltpu.VMEM((8, 2, 32, 1024), F32),
            pltpu.VMEM((8, 2, 32, 1024), F32),
            pltpu.VMEM((16, 32, 1024), BF16),
            pltpu.VMEM((16, 32, 1024), BF16),
            pltpu.VMEM((8, 2, 32, 1024), F32),
            dma((5,)),
            dma((18,)), dma((18,)),
            dma((16,)), dma((16,)),
            dma((8, 2, 4)), dma((8, 2, 4)),
            dma((8, 2, 4)), dma((8, 2, 4)),
            dma((2, 2, 4)), dma((2, 2, 4)),
            dma((8,)), dma((8,)),
            dma((16,)), dma((16,)),
        ],
        compiler_params=pltpu.CompilerParams(
            collective_id=0, has_side_effects=True, vmem_limit_bytes=56 * 2**20
        ),
    )(tokens, cotangent, gate_weight, up_weight, down_weight)
    return pl.pallas_call(
        flush,
        out_shape=tuple(jax.ShapeDtypeStruct(shape, BF16) for shape in shapes),
        in_specs=[vmem] * 4,
        out_specs=(hbm,) * 4,
        scratch_shapes=[dma((4,))],
        compiler_params=pltpu.CompilerParams(vmem_limit_bytes=8 * 2**20),
    )(*results)


def solution(mesh):
    placed = (P("row", "col"), P("row", "col"), P("col", "row"), P("col", "row"), P("row", "col"))
    return jax.shard_map(
        body,
        mesh=mesh,
        in_specs=placed,
        out_specs=(P("col", "row"), P("col", "row"), P("row", "col"), P("row", "col")),
        check_vma=False,
    )
```
